512 devices in a mesh: dp: 32 (over x, z), vocab: 16 (over y, core).
Axes of the slice: x: 4, y: 8, z: 8, core: 2. Of those that a mesh axis runs over, the one named last changes fastest.
Arguments:
- counts: int32 [32, 16, 32, 128, 128], P('dp', 'vocab'), may hold values from 0 to 5
- tile_doc: int32 [32, 16, 32], P('dp', 'vocab'), may hold values from 0 to 3, as said below
- tile_word: int32 [32, 16, 32], P('dp', 'vocab'), may hold values from 0 to 7, as said below
- tile_live: int32 [32, 16], P('dp', 'vocab'), may hold values from 1 to 32, as said below
- doc_init: float32 [16384, 512], P('dp'), may hold values from 0.5 to 20
- topic_word: float32 [16384, 512], P(('vocab', 'dp')), may hold values from 0.01 to 10
- topic_mass: float32 [512], replicated, may hold values from 20000 to 24000
- noise: float32 [16384, 512], P(('vocab', 'dp')), may hold values from -4 to 4
Outputs:
- doc_topic: float32 [16384, 512], P(('dp', 'vocab'))
- new_topic_word: float32 [16384, 512], P(('vocab', 'dp'))
The draws below stay inside these ranges and needn't reach their ends.
Inputs may be any that keep to these rules, and one draw needn't show every extreme that they name: `tile_doc`: the 32 slots of a device name every pair of a doc block and a word block exactly once, together with tile_word. `tile_word`: the 32 slots of a device name every pair of a doc block and a word block exactly once, together with tile_doc. Only the first tile_live slots of a device hold tiles; some device has all 32 slots live.
All inputs are finite; a program needn't handle non-finite values.
Results may differ from the reference program's by a relative error of at most 0.00065.
Values may be sent and summed in bfloat16 or wider, within the bound.
A program may use at most 64 MiB of HBM per device.

```python
import math
import jax
import jax.numpy as jnp
from jax import lax

TOPICS = 512
BLOCK = 128
DOC_BLOCKS = 4
WORD_BLOCKS = 8
ITERS = 3
SLOTS = 32
DOCS = 16384
WORDS = 16384
N_DP = 32
N_VOCAB = 16


def draw_counts(key, part):
    base_key = jax.random.fold_in(key, 37)
    row_index = jnp.arange(N_DP).astype(jnp.int32)
    upper = 2 + 4 * row_index // max(N_DP - 1, 1)
    raw_bits = jax.random.randint(base_key, (N_DP, N_VOCAB, SLOTS, BLOCK, BLOCK), 0, 1048576)
    return (raw_bits % upper[:, None, None, None, None]).astype(jnp.int32)


def pair_table(key):
    base_key = jax.random.fold_in(key, 11)
    device_keys = jax.random.split(base_key, N_DP * N_VOCAB)

    def one_order(single_key):
        return jax.random.permutation(single_key, SLOTS)
    orders = jax.vmap(one_order)(device_keys)
    return orders.reshape(N_DP, N_VOCAB, SLOTS).astype(jnp.int32)


def draw_tile_doc(key, part):
    return (pair_table(key) // WORD_BLOCKS).astype(jnp.int32)


def draw_tile_word(key, part):
    return (pair_table(key) % WORD_BLOCKS).astype(jnp.int32)


def draw_tile_live(key, part):
    base_key = jax.random.fold_in(key, 23)
    first_key, second_key, third_key = jax.random.split(base_key, 3)
    first = jax.random.randint(first_key, (N_DP * N_VOCAB,), 1, SLOTS + 1)
    second = jax.random.randint(second_key, (N_DP * N_VOCAB,), 1, SLOTS + 1)
    chosen = jax.random.randint(third_key, (), 0, N_DP * N_VOCAB)
    lowest = jnp.minimum(first, second)
    filled = jnp.where(jnp.arange(N_DP * N_VOCAB) == chosen, SLOTS, lowest)
    return filled.reshape(N_DP, N_VOCAB).astype(jnp.int32)


def draw_topic_word(key, part):
    base_key = jax.random.fold_in(key, 53)
    level_key, entry_key = jax.random.split(base_key)
    levels = jax.random.uniform(level_key, (WORDS // BLOCK, TOPICS), jnp.float32, -2.0, 2.0)
    spread_levels = jnp.repeat(levels, BLOCK, axis=0)
    entries = jax.random.uniform(entry_key, (WORDS, TOPICS), jnp.float32, -1.45, 1.45)
    return jnp.exp(-1.15 + spread_levels + entries).astype(jnp.float32)


def steps_of(stream_key, extent, cuts, smallest, top_value):
    level = 1.0
    for dim, shards_of in cuts:
        draws = jax.random.uniform(jax.random.fold_in(jax.random.fold_in(stream_key, 6), dim), (shards_of,), jnp.float32, smallest / len(cuts), top_value / len(cuts))
        level = level * jnp.repeat(jnp.exp(draws), extent[dim] // shards_of).reshape((-1,) + (1,) * (len(extent) - 1 - dim))
    return level


def normal_values(stream_key, extent, width, most, pieces=(), dtype=jnp.bfloat16):
    values = width * jax.random.normal(stream_key, extent, jnp.float32)
    if pieces:
        values = values * steps_of(stream_key, extent, pieces, -0.22, 0.18)
    return jnp.clip(values, -most, most).astype(dtype)


def setup_inputs(seed: int = 0) -> dict:
    key_of = jax.random.split(jax.random.key(seed), 9)
    counts = draw_counts(jax.random.fold_in(key_of[8], 71), 0)
    tile_doc = draw_tile_doc(jax.random.fold_in(key_of[8], 71), 0)
    tile_word = draw_tile_word(jax.random.fold_in(key_of[8], 71), 0)
    tile_live = draw_tile_live(jax.random.fold_in(key_of[8], 71), 0)
    doc_init = jnp.clip(jnp.exp(math.log(20.0) - 3.6888795 * jax.random.uniform(key_of[4], (DOCS, TOPICS), jnp.float32) ** steps_of(key_of[4], (DOCS, TOPICS), ((0, 32),), -0.2, 0.2)), 0.5, 20.0)
    topic_word = draw_topic_word(jax.random.fold_in(key_of[8], 71), 0)
    topic_mass = jnp.clip(jnp.exp(jax.random.uniform(key_of[6], (TOPICS,), jnp.float32, math.log(20000.0), math.log(24000.0))), 20000.0, 24000.0)
    noise = normal_values(key_of[7], (WORDS, TOPICS), 0.3, 4.0, ((0, 512),), jnp.float32)
    return dict(counts=counts, tile_doc=tile_doc, tile_word=tile_word, tile_live=tile_live, doc_init=doc_init, topic_word=topic_word, topic_mass=topic_mass, noise=noise)


ALPHA_PRIOR = 0.1
BETA_PRIOR = 0.01
HALF_STEP = 0.05
GRAD_SCALE = 16.0

def reference(counts, tile_doc, tile_word, tile_live, doc_init, topic_word, topic_mass, noise):
    topic_prob = topic_word / topic_mass[None, :]
    prob_blocks = topic_prob.astype(jnp.bfloat16).reshape(N_VOCAB, WORD_BLOCKS, BLOCK, TOPICS)
    slot_range = jnp.arange(SLOTS).astype(jnp.int32)
    live_mask = (slot_range[None, None, :] < tile_live[:, :, None]).astype(jnp.float32)
    doc_hot = (tile_doc[..., None] == jnp.arange(DOC_BLOCKS).astype(jnp.int32)).astype(jnp.float32)
    word_hot = (tile_word[..., None] == jnp.arange(WORD_BLOCKS).astype(jnp.int32)).astype(jnp.float32)
    panel_range = jnp.arange(N_VOCAB).astype(jnp.int32)[:, None]
    row_range = jnp.arange(N_DP).astype(jnp.int32)

    def row_ratios(row_index, gamma_rows):
        doc_rows = gamma_rows[tile_doc[row_index]]
        word_rows = prob_blocks[panel_range, tile_word[row_index]]
        rates = jnp.einsum('vsdk,vswk->vsdw', doc_rows.astype(jnp.float32), word_rows.astype(jnp.float32))
        ratios = (counts[row_index].astype(jnp.float32) / rates * live_mask[row_index][:, :, None, None]).astype(jnp.bfloat16)
        return (doc_rows, word_rows, ratios)
    doc_gamma = doc_init
    for iteration in range(ITERS):
        gamma_blocks = doc_gamma.astype(jnp.bfloat16).reshape(N_DP, DOC_BLOCKS, BLOCK, TOPICS)

        def row_sum(row_index):
            doc_rows, word_rows, ratios = row_ratios(row_index, gamma_blocks[row_index])
            partial_value = jnp.einsum('vsdw,vswk->vsdk', ratios.astype(jnp.float32), word_rows.astype(jnp.float32))
            return jnp.einsum('vsdk,vsc->cdk', partial_value, doc_hot[row_index], precision=lax.Precision.HIGHEST)
        summed = lax.map(row_sum, row_range)
        doc_gamma = ALPHA_PRIOR + doc_gamma * summed.reshape(DOCS, TOPICS)
    totals = lax.optimization_barrier(jnp.sum(doc_gamma - ALPHA_PRIOR, axis=0))
    gamma_blocks = doc_gamma.astype(jnp.bfloat16).reshape(N_DP, DOC_BLOCKS, BLOCK, TOPICS)

    def add_row(running, row_index):
        doc_rows, word_rows, ratios = row_ratios(row_index, gamma_blocks[row_index])
        partial_value = jnp.einsum('vsdw,vsdk->vswk', ratios.astype(jnp.float32), doc_rows.astype(jnp.float32))
        placed = jnp.einsum('vswk,vsa->vawk', partial_value, word_hot[row_index], precision=lax.Precision.HIGHEST)
        return (running + placed, None)
    word_hits, _ = lax.scan(add_row, jnp.zeros((N_VOCAB, WORD_BLOCKS, BLOCK, TOPICS), jnp.float32), row_range)
    word_hits = word_hits.reshape(WORDS, TOPICS)
    drift_term = BETA_PRIOR - topic_word + GRAD_SCALE * (topic_prob * word_hits - totals[None, :] * topic_prob)
    updated = jnp.abs(topic_word + HALF_STEP * drift_term + jnp.sqrt(topic_word) * noise)
    doc_topic = doc_gamma / (lax.optimization_barrier(jnp.sum(doc_gamma, axis=1, keepdims=True)) / TOPICS)
    return (doc_topic, updated)
```

```python
import functools

import jax
import jax.numpy as jnp
from jax import lax
from jax.experimental import pallas as pl
from jax.experimental.pallas import tpu as pltpu
from jax.sharding import PartitionSpec as P

ITERS = 3
ALPHA_PRIOR = 0.1
BETA_PRIOR = 0.01
HALF_STEP = 0.05
GRAD_SCALE = 16.0
MESH = pl.DeviceIdType.MESH
CHAINS = 2
X_CHIPS = 4


def far_first(count):
    return sorted(range(1, count), key=lambda j: -min(j, count - j))


def near_first(count):
    return sorted(range(1, count), key=lambda j: min(j, count - j))


def nt_dot(a, b):
    return lax.dot_general(a, b, (((1,), (1,)), ((), ())), preferred_element_type=jnp.float32)


def tn_dot(a, b):
    return lax.dot_general(a, b, (((0,), (0,)), ((), ())), preferred_element_type=jnp.float32)


def body(
    nx, nz, ny, share,
    slot_ref, counts_hbm, doc_hbm, word_ref, mass_ref, noise_ref,
    doc_out, word_out,
    cbuf, dbuf, cnt, cnt_sib, prob, gam_b, gam_sib, gam, part, got, hits, got_x, got_z,
    tot_y, tot_c, tot_x, tot_z,
    in_sem, doc_sem, cnt_sem,
    pz_s, pz_r, px_s, px_r, pc_s, pc_r,
    s_s, s_r, g_s, g_r, gc_s, gc_r,
    hx_s, hx_r, hz_s, hz_r,
    ty_s, ty_r, tc_s, tc_r, tx_s, tx_r, tz_s, tz_r,
):
    slots, block = counts_hbm.shape[0], counts_hbm.shape[1]
    panel = prob.shape[1]
    wblocks = panel // block
    rows_x = nz * share
    sub = share // CHAINS
    dp = lax.axis_index("dp")
    vo = lax.axis_index("vocab")
    x, z = dp // nz, lax.rem(dp, nz)
    y, c = vo // 2, lax.rem(vo, 2)
    sib = 1 - c

    def at_y(j):
        return (dp, lax.rem(y + j, ny) * 2 + c)

    def at_x(j):
        return (lax.rem(x + j, nx) * nz + z, vo)

    def at_z(j):
        return (x * nz + lax.rem(z + j, nz), vo)

    at_c = (dp, y * 2 + sib)

    def remote(src, dst, s, r, to):
        return pltpu.make_async_remote_copy(
            src_ref=src, dst_ref=dst, send_sem=s, recv_sem=r, device_id=to, device_id_type=MESH
        )

    counts_in = pltpu.make_async_copy(counts_hbm, cbuf.at[pl.ds(0, slots)], in_sem)
    counts_in.start()
    doc_in = [
        pltpu.make_async_copy(
            doc_hbm.at[pl.ds((2 * q + c) * share, share)], dbuf.at[q], doc_sem.at[q]
        )
        for q in range(ny)
    ]
    for copy in doc_in:
        copy.start()

    barrier = pltpu.get_barrier_semaphore()
    peers = [at_y(j) for j in range(1, ny)] + [at_c]
    peers += [at_x(j) for j in range(1, nx)] + [at_z(j) for j in range(1, nz)]
    for to in peers:
        pl.semaphore_signal(barrier, inc=1, device_id=to, device_id_type=MESH)

    prob_own = word_ref[...] / mass_ref[...]

    def shard(jx, jz):
        row = (lax.rem(x - jx + nx, nx) * nz + lax.rem(z - jz + nz, nz)) * share
        return prob.at[c, pl.ds(pl.multiple_of(row, share), share)]

    def xblock(jx):
        row = lax.rem(x - jx + nx, nx) * rows_x
        return prob.at[c, pl.ds(pl.multiple_of(row, rows_x), rows_x)]

    def sib_xblock(jx):
        row = lax.rem(x - jx + nx, nx) * rows_x
        return prob.at[sib, pl.ds(pl.multiple_of(row, rows_x), rows_x)]

    shard(0, 0)[...] = prob_own.astype(jnp.bfloat16)
    pl.semaphore_wait(barrier, len(peers))

    pz = {j: remote(shard(0, 0), shard(0, 0), pz_s.at[j], pz_r.at[j], at_z(j)) for j in range(1, nz)}
    px = {
        (jx, jz): remote(shard(0, jz), shard(0, jz), px_s.at[jx, jz], px_r.at[jx, jz], at_x(jx))
        for jx in range(1, nx)
        for jz in range(nz)
    }
    for j in far_first(nz):
        pz[j].start()
    for jx in far_first(nx):
        px[jx, 0].start()

    counts_in.wait()
    cbuf[slots] = jnp.zeros((block, block), jnp.int32)
    per_block = block // share
    pairs = per_block // 2 if per_block > 1 else 1

    def place(t, _):
        d, w = t // wblocks, lax.rem(t, wblocks)
        slot = slot_ref[t]
        col = pl.ds(pl.multiple_of(w * block, block), block)
        for k in range(pairs):
            for other in range(2):
                core = sib if other else c
                piece = cbuf[slot, pl.ds(pl.multiple_of((2 * k + core) * share, share), share), :]
                piece = piece.astype(jnp.float32).astype(jnp.bfloat16)
                for h in range(CHAINS):
                    row = pl.ds(pl.multiple_of((d * pairs + k) * sub, sub), sub)
                    val = piece[h * sub:(h + 1) * sub]
                    if other:
                        cnt_sib[h, row, col] = val
                    else:
                        cnt[c, h, row, col] = val
        return 0

    lax.fori_loop(0, slots, place, 0)
    cnt_go = remote(cnt_sib, cnt.at[c], cnt_sem.at[0], cnt_sem.at[1], at_c)
    cnt_go.start()

    for copy in doc_in:
        copy.wait()
    for h in range(CHAINS):
        for q in range(ny):
            gam_b[h, q * sub:(q + 1) * sub, :] = dbuf[q, h * sub:(h + 1) * sub, :].astype(jnp.bfloat16)
        gam[h] = dbuf[y, h * sub:(h + 1) * sub, :]

    for jz in near_first(nz):
        remote(shard(0, jz), shard(0, jz), pz_s.at[jz], pz_r.at[jz], at_z(jz)).wait_recv()
        for jx in far_first(nx):
            px[jx, jz].start()
    pc = [remote(xblock(jx), xblock(jx), pc_s.at[jx], pc_r.at[jx], at_c) for jx in range(nx)]
    pc[0].start()
    for jx in near_first(nx):
        for jz in [0] + near_first(nz):
            remote(shard(jx, jz), shard(jx, jz), px_s.at[jx, jz], px_r.at[jx, jz], at_x(jx)).wait_recv()
        pc[jx].start()
    remote(cnt_sib, cnt.at[sib], cnt_sem.at[0], cnt_sem.at[1], at_c).wait_recv()
    for jx in range(nx):
        remote(sib_xblock(jx), sib_xblock(jx), pc_s.at[jx], pc_r.at[jx], at_c).wait_recv()

    chunk = min(512, panel)
    per_panel = panel // chunk

    def partial_sums(h):
        part[h] = jnp.zeros(part.shape[1:], jnp.float32)

        def step(t, _):
            side, k = t // per_panel, lax.rem(t, per_panel)
            words = pl.ds(pl.multiple_of(k * chunk, chunk), chunk)
            p = prob[side, words, :]
            rates = nt_dot(gam_b[h], p)
            ratios = (cnt[side, h, :, words].astype(jnp.float32) / rates).astype(jnp.bfloat16)
            part[h] += jnp.dot(ratios, p, preferred_element_type=jnp.float32)
            return 0

        lax.fori_loop(0, 2 * per_panel, step, 0)

    def doc_rows(j):
        return pl.ds(pl.multiple_of(lax.rem(y + j + ny, ny) * sub, sub), sub)

    def send_sums(h, j):
        return remote(part.at[h, doc_rows(j)], got.at[h, j], s_s.at[h, j], s_r.at[h, j], at_y(j))

    def send_gamma(h, j):
        own = gam_b.at[h, doc_rows(0)]
        return remote(own, own, g_s.at[h, j], g_r.at[h, j], at_y(j))

    def wait_gamma(h, j):
        theirs = gam_b.at[h, doc_rows(-j)]
        remote(theirs, theirs, g_s.at[h, j], g_r.at[h, j], at_y(j)).wait_recv()

    for it in range(ITERS):
        for h in range(CHAINS):
            if it:
                for j in near_first(ny):
                    wait_gamma(h, j)
                for j in range(1, ny):
                    send_sums(h, j).wait_send()
            partial_sums(h)
            for j in far_first(ny):
                send_sums(h, j).start()
        for h in range(CHAINS):
            total = part[h, doc_rows(0), :]
            for j in near_first(ny):
                send_sums(h, j).wait_recv()
                total = total + got[h, j]
            gam[h] = ALPHA_PRIOR + gam[h] * total
            if it:
                for j in range(1, ny):
                    send_gamma(h, j).wait_send()
            gam_b[h, doc_rows(0), :] = gam[h].astype(jnp.bfloat16)
            for j in far_first(ny):
                send_gamma(h, j).start()

    final = jnp.concatenate([gam[h] for h in range(CHAINS)], axis=0)
    tot_y[0] = jnp.sum(final - ALPHA_PRIOR, axis=0, keepdims=True)

    def send_ty(j):
        return remote(tot_y.at[0], tot_y.at[j], ty_s.at[j], ty_r.at[j], at_y(j))

    for j in far_first(ny):
        send_ty(j).start()
    topics = final.shape[1]
    doc_out[...] = final / (jnp.sum(final, axis=1, keepdims=True) / topics)

    def give(h):
        return remote(gam_b.at[h], gam_sib.at[h], gc_s.at[h], gc_r.at[h], at_c)

    for h in range(CHAINS):
        for j in near_first(ny):
            wait_gamma(h, j)
        give(h).start()
    total = tot_y[0]
    for j in near_first(ny):
        send_ty(j).wait_recv()
        total = total + tot_y[j]
    tot_c[0] = total
    send_tc = remote(tot_c.at[0], tot_c.at[1], tc_s, tc_r, at_c)
    send_tc.start()
    for h in range(CHAINS):
        give(h).wait_recv()
    send_tc.wait_recv()
    tot_x[0] = tot_c[0] + tot_c[1]

    def send_tx(j):
        return remote(tot_x.at[0], tot_x.at[j], tx_s.at[j], tx_r.at[j], at_x(j))

    for j in far_first(nx):
        send_tx(j).start()

    def send_hx(j):
        return remote(hits.at[j], got_x.at[j], hx_s.at[j], hx_r.at[j], at_x(j))

    for j in far_first(nx) + [0]:
        words = pl.ds(pl.multiple_of(lax.rem(x + j, nx) * rows_x, rows_x), rows_x)
        p = prob[c, words, :]
        for h in range(CHAINS):
            for other in range(2):
                g = gam_sib[h] if other else gam_b[h]
                n = cnt_sib[h, :, words] if other else cnt[c, h, :, words]
                ratios = (n.astype(jnp.float32) / nt_dot(g, p)).astype(jnp.bfloat16)
                add = tn_dot(ratios, g)
                if h == 0 and other == 0:
                    hits[j] = add
                else:
                    hits[j] += add
        if j:
            send_hx(j).start()

    total = tot_x[0]
    for j in near_first(nx):
        send_tx(j).wait_recv()
        total = total + tot_x[j]
    tot_z[0] = total

    def send_tz(j):
        return remote(tot_z.at[0], tot_z.at[j], tz_s.at[j], tz_r.at[j], at_z(j))

    for j in far_first(nz):
        send_tz(j).start()
    for j in near_first(nx):
        send_hx(j).wait_recv()

    def z_rows(j):
        return pl.ds(pl.multiple_of(lax.rem(z + j, nz) * share, share), share)

    def send_hz(j):
        return remote(hits.at[0, z_rows(j)], got_z.at[j], hz_s.at[j], hz_r.at[j], at_z(j))

    for j in far_first(nz) + [0]:
        total = hits[0, z_rows(j), :]
        for jx in range(1, nx):
            total = total + got_x[jx, z_rows(j), :]
        hits[0, z_rows(j), :] = total
        if j:
            send_hz(j).start()

    total = tot_z[0]
    for j in near_first(nz):
        send_tz(j).wait_recv()
        total = total + tot_z[j]
    totals = total
    reduced = hits[0, z_rows(0), :]
    for j in near_first(nz):
        send_hz(j).wait_recv()
        reduced = reduced + got_z[j]
    word = word_ref[...]
    probs = word / mass_ref[...]
    drift = BETA_PRIOR - word + GRAD_SCALE * (probs * reduced - totals * probs)
    word_out[...] = jnp.abs(word + HALF_STEP * drift + jnp.sqrt(word) * noise_ref[...])

    for j in range(1, nz):
        pz[j].wait_send()
        send_hz(j).wait_send()
        send_tz(j).wait_send()
    for jx in range(1, nx):
        send_hx(jx).wait_send()
        send_tx(jx).wait_send()
        for jz in range(nz):
            px[jx, jz].wait_send()
    for jx in range(nx):
        pc[jx].wait_send()
    cnt_go.wait_send()
    send_tc.wait_send()
    for h in range(CHAINS):
        give(h).wait_send()
        for j in range(1, ny):
            send_sums(h, j).wait_send()
            send_gamma(h, j).wait_send()
    for j in range(1, ny):
        send_ty(j).wait_send()


def shards(counts, tile_doc, tile_word, tile_live, doc_init, topic_word, topic_mass, noise):
    topics = topic_mass.shape[0]
    slots, block = counts.shape[2], counts.shape[3]
    n_dp, n_vocab = lax.axis_size("dp"), lax.axis_size("vocab")
    nx = X_CHIPS
    nz, ny = n_dp // nx, n_vocab // 2
    share = topic_word.shape[0]
    panel = share * n_dp
    sub = share // CHAINS
    docs = ny * sub
    wblocks = panel // block

    order = jnp.arange(slots, dtype=jnp.int32)
    key = tile_doc[0, 0] * wblocks + tile_word[0, 0]
    usable = jnp.where(order < tile_live[0, 0], order, slots)
    slot_of = jnp.sum(jnp.where(key[None, :] == order[:, None], usable[None, :], 0), axis=1)

    f32, bf16, dma = jnp.float32, jnp.bfloat16, pltpu.SemaphoreType.DMA
    vmem = pl.BlockSpec(memory_space=pltpu.VMEM)
    return pl.pallas_call(
        functools.partial(body, nx, nz, ny, share),
        out_shape=(
            jax.ShapeDtypeStruct((share, topics), f32),
            jax.ShapeDtypeStruct((share, topics), f32),
        ),
        in_specs=[
            pl.BlockSpec(memory_space=pltpu.SMEM),
            pl.BlockSpec(memory_space=pl.ANY),
            pl.BlockSpec(memory_space=pl.ANY),
            vmem, vmem, vmem,
        ],
        out_specs=(vmem, vmem),
        scratch_shapes=[
            pltpu.VMEM((slots + 1, block, block), jnp.int32),
            pltpu.VMEM((ny, share, topics), f32),
            pltpu.VMEM((2, CHAINS, docs, panel), bf16),
            pltpu.VMEM((CHAINS, docs, panel), bf16),
            pltpu.VMEM((2, panel, topics), bf16),
            pltpu.VMEM((CHAINS, docs, topics), bf16),
            pltpu.VMEM((CHAINS, docs, topics), bf16),
            pltpu.VMEM((CHAINS, sub, topics), f32),
            pltpu.VMEM((CHAINS, docs, topics), f32),
            pltpu.VMEM((CHAINS, ny, sub, topics), f32),
            pltpu.VMEM((nx, nz * share, topics), f32),
            pltpu.VMEM((nx, nz * share, topics), f32),
            pltpu.VMEM((nz, share, topics), f32),
            pltpu.VMEM((ny, 1, topics), f32),
            pltpu.VMEM((2, 1, topics), f32),
            pltpu.VMEM((nx, 1, topics), f32),
            pltpu.VMEM((nz, 1, topics), f32),
            dma, dma((ny,)), dma((2,)),
            dma((nz,)), dma((nz,)), dma((nx, nz)), dma((nx, nz)), dma((nx,)), dma((nx,)),
            dma((CHAINS, ny)), dma((CHAINS, ny)), dma((CHAINS, ny)), dma((CHAINS, ny)),
            dma((CHAINS,)), dma((CHAINS,)),
            dma((nx,)), dma((nx,)), dma((nz,)), dma((nz,)),
            dma((ny,)), dma((ny,)), dma, dma, dma((nx,)), dma((nx,)), dma((nz,)), dma((nz,)),
        ],
        compiler_params=pltpu.CompilerParams(
            collective_id=0, has_side_effects=True, vmem_limit_bytes=48 * 2**20
        ),
    )(slot_of, counts[0, 0], doc_init, topic_word, topic_mass[None, :], noise)


def solution(mesh):
    return jax.shard_map(
        shards,
        mesh=mesh,
        in_specs=(
            P("dp", "vocab", None, None, None),
            P("dp", "vocab", None),
            P("dp", "vocab", None),
            P("dp", "vocab"),
            P("dp", None),
            P(("vocab", "dp"), None),
            P(),
            P(("vocab", "dp"), None),
        ),
        out_specs=(P(("dp", "vocab"), None), P(("vocab", "dp"), None)),
        check_vma=False,
    )
```

```python
import functools

import jax
import jax.numpy as jnp
from jax import lax
from jax.experimental import pallas as pl
from jax.experimental.pallas import tpu as pltpu
from jax.sharding import PartitionSpec as P

ITERS = 3
ALPHA_PRIOR = 0.1
BETA_PRIOR = 0.01
HALF_STEP = 0.05
GRAD_SCALE = 16.0
MESH = pl.DeviceIdType.MESH
CHAINS = 2
X_CHIPS = 4
VMEM_LIMIT = 58 * 2**20


def far_first(count):
    return sorted(range(1, count), key=lambda j: -min(j, count - j))


def near_first(count):
    return sorted(range(1, count), key=lambda j: min(j, count - j))


def nt_dot(a, b):
    return lax.dot_general(a, b, (((1,), (1,)), ((), ())), preferred_element_type=jnp.float32)


def body(
    nx, nz, ny, share,
    doc_pick, word_pick, live, counts_hbm, doc_hbm, word_hbm, mass_hbm, noise_hbm,
    doc_out, word_out,
    slot_vm, slot_ref, cbuf, dbuf, word_ref, mass_ref, noise_ref,
    cnt, cnt_sib, cnt_t, prob, gall, gam, part, got, hits, got_x, got_z,
    tot_y, tot_c, tot_x, tot_z,
    in_sem, doc_sem, cnt_sem,
    pz_s, pz_r, px_s, px_r, pc_s, pc_r,
    s_s, s_r, g_s, g_r, gc_s, gc_r,
    hx_s, hx_r, hz_s, hz_r,
    ty_s, ty_r, tc_s, tc_r, tx_s, tx_r, tz_s, tz_r,
):
    slots, block = counts_hbm.shape[2], counts_hbm.shape[3]
    panel, topics = prob.shape[1], prob.shape[2]
    wblocks = panel // block
    rows_x = nz * share
    sub = share // CHAINS
    docs = ny * sub
    dp = lax.axis_index("dp")
    vo = lax.axis_index("vocab")
    x, z = dp // nz, lax.rem(dp, nz)
    y, c = vo // 2, lax.rem(vo, 2)
    sib = 1 - c

    def at_y(j):
        return (dp, lax.rem(y + j, ny) * 2 + c)

    def at_x(j):
        return (lax.rem(x + j, nx) * nz + z, vo)

    def at_z(j):
        return (x * nz + lax.rem(z + j, nz), vo)

    at_c = (dp, y * 2 + sib)

    def remote(src, dst, s, r, to):
        return pltpu.make_async_remote_copy(
            src_ref=src, dst_ref=dst, send_sem=s, recv_sem=r, device_id=to, device_id_type=MESH
        )

    word_in = pltpu.make_async_copy(word_hbm, word_ref, in_sem.at[0])
    mass_in = pltpu.make_async_copy(mass_hbm, mass_ref, in_sem.at[1])
    word_in.start()
    mass_in.start()

    barrier = pltpu.get_barrier_semaphore()
    peers = [at_y(j) for j in range(1, ny)] + [at_c]
    peers += [at_x(j) for j in range(1, nx)] + [at_z(j) for j in range(1, nz)]
    for to in peers:
        pl.semaphore_signal(barrier, inc=1, device_id=to, device_id_type=MESH)

    counts_in = pltpu.make_async_copy(counts_hbm.at[0, 0], cbuf.at[pl.ds(0, slots)], in_sem.at[2])
    counts_in.start()
    doc_in = [
        pltpu.make_async_copy(
            doc_hbm.at[pl.ds((2 * q + c) * share, share)], dbuf.at[q], doc_sem.at[q]
        )
        for q in range(ny)
    ]
    for copy in doc_in:
        copy.start()
    noise_in = pltpu.make_async_copy(noise_hbm, noise_ref, in_sem.at[3])
    noise_in.start()

    lane = lax.broadcasted_iota(jnp.int32, (1, 128), 1)
    slot_of = jnp.full((1, 128), slots, jnp.int32)
    for s in range(slots):
        key = doc_pick[0, 0, s] * wblocks + word_pick[0, 0, s]
        use = jnp.where(s < live[0, 0], s, slots)
        slot_of = jnp.where(lane == key, use, slot_of)
    slot_vm[...] = slot_of
    slot_in = pltpu.make_async_copy(slot_vm, slot_ref, in_sem.at[4])
    slot_in.start()

    def word_rows(jx, jz):
        row = (lax.rem(x - jx + nx, nx) * nz + lax.rem(z - jz + nz, nz)) * share
        return pl.ds(pl.multiple_of(row, share), share)

    def word_block(jx):
        return pl.ds(pl.multiple_of(lax.rem(x - jx + nx, nx) * rows_x, rows_x), rows_x)

    def shard(jx, jz):
        return prob.at[c, word_rows(jx, jz)]

    word_in.wait()
    mass_in.wait()
    prob[c, word_rows(0, 0), :] = (word_ref[...] / mass_ref[...]).astype(jnp.bfloat16)
    pl.semaphore_wait(barrier, len(peers))

    pz = {j: remote(shard(0, 0), shard(0, 0), pz_s.at[j], pz_r.at[j], at_z(j)) for j in range(1, nz)}
    px = {
        (jx, jz): remote(shard(0, jz), shard(0, jz), px_s.at[jx, jz], px_r.at[jx, jz], at_x(jx))
        for jx in range(1, nx)
        for jz in range(nz)
    }
    pc = [
        remote(prob.at[c, word_block(jx)], prob.at[c, word_block(jx)], pc_s.at[jx], pc_r.at[jx], at_c)
        for jx in range(nx)
    ]
    for j in near_first(nz):
        pz[j].start()
    for jx in far_first(nx):
        px[jx, 0].start()

    for copy in doc_in:
        copy.wait()
    for h in range(CHAINS):
        for q in range(ny):
            gall[q, c, h] = dbuf[q, h * sub:(h + 1) * sub, :].astype(jnp.bfloat16)
        gam[h] = dbuf[y, h * sub:(h + 1) * sub, :]

    for jz in near_first(nz):
        remote(shard(0, jz), shard(0, jz), pz_s.at[jz], pz_r.at[jz], at_z(jz)).wait_recv()
        for jx in far_first(nx):
            px[jx, jz].start()
    pc[0].start()

    counts_in.wait()
    slot_in.wait()
    cbuf[slots] = jnp.zeros((block, block), jnp.int32)
    pairs = block // share // 2

    def place(t, _):
        d, w = t // wblocks, lax.rem(t, wblocks)
        slot = slot_ref[0, t]
        col = pl.ds(pl.multiple_of(w * block, block), block)
        for k in range(pairs):
            for other in range(2):
                core = sib if other else c
                piece = cbuf[slot, pl.ds(pl.multiple_of((2 * k + core) * share, share), share), :]
                piece = piece.astype(jnp.float32).astype(jnp.bfloat16)
                for h in range(CHAINS):
                    row = pl.ds(pl.multiple_of((d * pairs + k) * sub, sub), sub)
                    val = piece[h * sub:(h + 1) * sub]
                    if other:
                        cnt_sib[h, row, col] = val
                    else:
                        cnt[c, h, row, col] = val
        return 0

    lax.fori_loop(0, slots, place, 0)
    cnt_go = remote(cnt_sib, cnt.at[c], cnt_sem.at[0], cnt_sem.at[1], at_c)
    cnt_go.start()

    def turn(w, _):
        row = pl.ds(pl.multiple_of(w * block, block), block)
        for d in range(slots // wblocks):
            tile = cbuf[slot_ref[0, d * wblocks + w]].astype(jnp.float32)
            cnt_t[row, d * block:(d + 1) * block] = tile.T.astype(jnp.bfloat16)
        return 0

    lax.fori_loop(0, wblocks, turn, 0)

    def chain_gamma(h):
        return jnp.concatenate([gall[q, c, h] for q in range(ny)], axis=0)

    both = jnp.concatenate([chain_gamma(h) for h in range(CHAINS)], axis=0)

    def first_sums(side, jx, first):
        words = word_block(jx)
        p = prob[side, words, :]
        n = jnp.concatenate([cnt[side, h, :, words] for h in range(CHAINS)], axis=0)
        ratios = (n.astype(jnp.float32) / nt_dot(both, p)).astype(jnp.bfloat16)
        add = jnp.dot(ratios, p, preferred_element_type=jnp.float32)
        for h in range(CHAINS):
            if first:
                part[h] = add[h * docs:(h + 1) * docs]
            else:
                part[h] += add[h * docs:(h + 1) * docs]

    def sib_sums(jx):
        theirs = prob.at[sib, word_block(jx)]
        remote(theirs, theirs, pc_s.at[jx], pc_r.at[jx], at_c).wait_recv()
        first_sums(sib, jx, False)

    first_sums(c, 0, True)
    remote(cnt_sib, cnt.at[sib], cnt_sem.at[0], cnt_sem.at[1], at_c).wait_recv()
    sib_sums(0)
    before = None
    for jx in near_first(nx):
        for jz in [0] + near_first(nz):
            remote(shard(jx, jz), shard(jx, jz), px_s.at[jx, jz], px_r.at[jx, jz], at_x(jx)).wait_recv()
        pc[jx].start()
        first_sums(c, jx, False)
        if before is not None:
            sib_sums(before)
        before = jx
    sib_sums(before)

    chunk = min(512, panel)

    def partial_sums(h):
        g = chain_gamma(h)
        total = None
        for side in range(2):
            for k in range(panel // chunk):
                words = pl.ds(k * chunk, chunk)
                p = prob[side, words, :]
                n = cnt[side, h, :, words].astype(jnp.float32)
                ratios = (n / nt_dot(g, p)).astype(jnp.bfloat16)
                add = jnp.dot(ratios, p, preferred_element_type=jnp.float32)
                total = add if total is None else total + add
        part[h] = total

    def doc_rows(j):
        return pl.ds(pl.multiple_of(lax.rem(y + j + ny, ny) * sub, sub), sub)

    def send_sums(h, j):
        return remote(part.at[h, doc_rows(j)], got.at[h, j], s_s.at[h, j], s_r.at[h, j], at_y(j))

    def send_gamma(h, j):
        own = gall.at[y, c, h]
        return remote(own, own, g_s.at[h, j], g_r.at[h, j], at_y(j))

    def wait_gamma(h, j):
        theirs = gall.at[lax.rem(y - j + ny, ny), c, h]
        remote(theirs, theirs, g_s.at[h, j], g_r.at[h, j], at_y(j)).wait_recv()

    for it in range(ITERS):
        for h in range(CHAINS):
            if it:
                for j in near_first(ny):
                    wait_gamma(h, j)
                for j in range(1, ny):
                    send_sums(h, j).wait_send()
                partial_sums(h)
            for j in far_first(ny):
                send_sums(h, j).start()
        for h in range(CHAINS):
            total = part[h, doc_rows(0), :]
            for j in near_first(ny):
                send_sums(h, j).wait_recv()
                total = total + got[h, j]
            gam[h] = ALPHA_PRIOR + gam[h] * total
            if it:
                for j in range(1, ny):
                    send_gamma(h, j).wait_send()
            gall[y, c, h] = gam[h].astype(jnp.bfloat16)
            for j in far_first(ny):
                send_gamma(h, j).start()

    final = jnp.concatenate([gam[h] for h in range(CHAINS)], axis=0)
    tot_y[0] = jnp.sum(final - ALPHA_PRIOR, axis=0, keepdims=True)

    def send_ty(j):
        return remote(tot_y.at[0], tot_y.at[j], ty_s.at[j], ty_r.at[j], at_y(j))

    for j in far_first(ny):
        send_ty(j).start()
    doc_out[...] = final / (jnp.sum(final, axis=1, keepdims=True) / topics)

    def give(h):
        mine = gall.at[:, c, h]
        return remote(mine, mine, gc_s.at[h], gc_r.at[h], at_c)

    def wait_give(h):
        theirs = gall.at[:, sib, h]
        remote(theirs, theirs, gc_s.at[h], gc_r.at[h], at_c).wait_recv()

    for h in range(CHAINS):
        for j in near_first(ny):
            wait_gamma(h, j)
        give(h).start()
    total = tot_y[0]
    for j in near_first(ny):
        send_ty(j).wait_recv()
        total = total + tot_y[j]
    tot_c[0] = total
    send_tc = remote(tot_c.at[0], tot_c.at[1], tc_s, tc_r, at_c)
    send_tc.start()
    for h in range(CHAINS):
        wait_give(h)

    def z_rows(j):
        return pl.ds(pl.multiple_of(lax.rem(z + j, nz) * share, share), share)

    def send_hx(jx, jz):
        return remote(
            hits.at[jx, z_rows(jz)], got_x.at[jx, z_rows(jz)],
            hx_s.at[jx, jz], hx_r.at[jx, jz], at_x(jx),
        )

    def send_hz(j):
        return remote(hits.at[0, z_rows(j)], got_z.at[j], hz_s.at[j], hz_r.at[j], at_z(j))

    def send_tx(j):
        return remote(tot_x.at[0], tot_x.at[j], tx_s.at[j], tx_r.at[j], at_x(j))

    def send_tz(j):
        return remote(tot_z.at[0], tot_z.at[j], tz_s.at[j], tz_r.at[j], at_z(j))

    gamma_all = gall[...].reshape(2 * CHAINS * docs, topics)
    z_order = far_first(nz) + [0]
    for jx in far_first(nx) + [0]:
        words = word_block(nx - jx)
        rates = nt_dot(prob[c, words, :], gamma_all)
        ratios = (cnt_t[words, :].astype(jnp.float32) / rates).astype(jnp.bfloat16)
        hits[jx] = jnp.dot(ratios, gamma_all, preferred_element_type=jnp.float32)
        if jx:
            for jz in z_order:
                send_hx(jx, jz).start()

    send_tc.wait_recv()
    tot_x[0] = tot_c[0] + tot_c[1]
    for j in far_first(nx):
        send_tx(j).start()
    total = tot_x[0]
    for j in near_first(nx):
        send_tx(j).wait_recv()
        total = total + tot_x[j]
    tot_z[0] = total
    for j in far_first(nz):
        send_tz(j).start()

    for jz in z_order:
        total = hits[0, z_rows(jz), :]
        for jx in range(1, nx):
            send_hx(jx, jz).wait_recv()
            total = total + got_x[jx, z_rows(jz), :]
        hits[0, z_rows(jz), :] = total
        if jz:
            send_hz(jz).start()

    totals = tot_z[0]
    for j in near_first(nz):
        send_tz(j).wait_recv()
        totals = totals + tot_z[j]
    noise_in.wait()
    reduced = hits[0, z_rows(0), :]
    for j in near_first(nz):
        send_hz(j).wait_recv()
        reduced = reduced + got_z[j]
    word = word_ref[...]
    probs = word / mass_ref[...]
    drift = BETA_PRIOR - word + GRAD_SCALE * (probs * reduced - totals * probs)
    word_out[...] = jnp.abs(word + HALF_STEP * drift + jnp.sqrt(word) * noise_ref[...])

    for j in range(1, nz):
        pz[j].wait_send()
        send_hz(j).wait_send()
        send_tz(j).wait_send()
    for jx in range(1, nx):
        send_tx(jx).wait_send()
        for jz in range(nz):
            px[jx, jz].wait_send()
            send_hx(jx, jz).wait_send()
    for jx in range(nx):
        pc[jx].wait_send()
    cnt_go.wait_send()
    send_tc.wait_send()
    for h in range(CHAINS):
        give(h).wait_send()
        for j in range(1, ny):
            send_sums(h, j).wait_send()
            send_gamma(h, j).wait_send()
    for j in range(1, ny):
        send_ty(j).wait_send()


def shards(counts, tile_doc, tile_word, tile_live, doc_init, topic_word, topic_mass, noise):
    topics = topic_mass.shape[0]
    slots, block = counts.shape[2], counts.shape[3]
    n_dp, n_vocab = lax.axis_size("dp"), lax.axis_size("vocab")
    nx = X_CHIPS
    nz, ny = n_dp // nx, n_vocab // 2
    share = topic_word.shape[0]
    panel = share * n_dp
    sub = share // CHAINS
    docs = ny * sub

    f32, bf16, dma = jnp.float32, jnp.bfloat16, pltpu.SemaphoreType.DMA
    vmem = pl.BlockSpec(memory_space=pltpu.VMEM)
    smem = pl.BlockSpec(memory_space=pltpu.SMEM)
    hbm = pl.BlockSpec(memory_space=pl.ANY)
    return pl.pallas_call(
        functools.partial(body, nx, nz, ny, share),
        out_shape=(
            jax.ShapeDtypeStruct((share, topics), f32),
            jax.ShapeDtypeStruct((share, topics), f32),
        ),
        in_specs=[smem, smem, smem, hbm, hbm, hbm, hbm, hbm],
        out_specs=(vmem, vmem),
        scratch_shapes=[
            pltpu.VMEM((1, 128), jnp.int32),
            pltpu.SMEM((1, 128), jnp.int32),
            pltpu.VMEM((slots + 1, block, block), jnp.int32),
            pltpu.VMEM((ny, share, topics), f32),
            pltpu.VMEM((share, topics), f32),
            pltpu.VMEM((1, topics), f32),
            pltpu.VMEM((share, topics), f32),
            pltpu.VMEM((2, CHAINS, docs, panel), bf16),
            pltpu.VMEM((CHAINS, docs, panel), bf16),
            pltpu.VMEM((panel, 2 * CHAINS * docs), bf16),
            pltpu.VMEM((2, panel, topics), bf16),
            pltpu.VMEM((ny, 2, CHAINS, sub, topics), bf16),
            pltpu.VMEM((CHAINS, sub, topics), f32),
            pltpu.VMEM((CHAINS, docs, topics), f32),
            pltpu.VMEM((CHAINS, ny, sub, topics), f32),
            pltpu.VMEM((nx, nz * share, topics), f32),
            pltpu.VMEM((nx, nz * share, topics), f32),
            pltpu.VMEM((nz, share, topics), f32),
            pltpu.VMEM((ny, 1, topics), f32),
            pltpu.VMEM((2, 1, topics), f32),
            pltpu.VMEM((nx, 1, topics), f32),
            pltpu.VMEM((nz, 1, topics), f32),
            dma((5,)), dma((ny,)), dma((2,)),
            dma((nz,)), dma((nz,)), dma((nx, nz)), dma((nx, nz)), dma((nx,)), dma((nx,)),
            dma((CHAINS, ny)), dma((CHAINS, ny)), dma((CHAINS, ny)), dma((CHAINS, ny)),
            dma((CHAINS,)), dma((CHAINS,)),
            dma((nx, nz)), dma((nx, nz)), dma((nz,)), dma((nz,)),
            dma((ny,)), dma((ny,)), dma, dma, dma((nx,)), dma((nx,)), dma((nz,)), dma((nz,)),
        ],
        compiler_params=pltpu.CompilerParams(
            collective_id=0, has_side_effects=True, vmem_limit_bytes=VMEM_LIMIT
        ),
    )(tile_doc, tile_word, tile_live, counts, doc_init, topic_word, topic_mass[None, :], noise)


def solution(mesh):
    return jax.shard_map(
        shards,
        mesh=mesh,
        in_specs=(
            P("dp", "vocab", None, None, None),
            P("dp", "vocab", None),
            P("dp", "vocab", None),
            P("dp", "vocab"),
            P("dp", None),
            P(("vocab", "dp"), None),
            P(),
            P(("vocab", "dp"), None),
        ),
        out_specs=(P(("dp", "vocab"), None), P(("vocab", "dp"), None)),
        check_vma=False,
    )
```

```python
import functools

import jax
import jax.numpy as jnp
from jax import lax
from jax.experimental import pallas as pl
from jax.experimental.pallas import tpu as pltpu
from jax.sharding import PartitionSpec as P

ITERS = 3
ALPHA_PRIOR = 0.1
BETA_PRIOR = 0.01
HALF_STEP = 0.05
GRAD_SCALE = 16.0
MESH = pl.DeviceIdType.MESH
CHAINS = 2
CODES = 65535.0
SCALE_STEPS = 1024.0
X_CHIPS = 4
VMEM_LIMIT = 58 * 2**20


def far_first(count):
    return sorted(range(1, count), key=lambda j: -min(j, count - j))


def near_first(count):
    return sorted(range(1, count), key=lambda j: min(j, count - j))


def nt_dot(a, b):
    return lax.dot_general(a, b, (((1,), (1,)), ((), ())), preferred_element_type=jnp.float32)


def pack(values):
    half = values.shape[0] // 2
    top = jnp.maximum(jnp.max(values, axis=0, keepdims=True), 1e-30)
    scale = (jnp.log2(top) * SCALE_STEPS + 1.0).astype(jnp.int32)
    factor = jnp.exp2(scale.astype(jnp.float32) * (-1.0 / SCALE_STEPS)) * CODES
    code = jnp.minimum(values * factor + 0.5, CODES).astype(jnp.int32)
    return code[:half] | (code[half:] << 16), scale


def store_packed(ref, values):
    half = values.shape[0] // 2
    code, scale = pack(values)
    ref[0:half, :] = code
    ref[half:half + 1, :] = scale


def unpack(ref):
    half = ref.shape[0] - 1
    code, scale = ref[0:half, :], ref[half:half + 1, :]
    unit = jnp.exp2(scale.astype(jnp.float32) * (1.0 / SCALE_STEPS)) * (1.0 / CODES)
    both = jnp.concatenate([code & 0xFFFF, (code >> 16) & 0xFFFF], axis=0)
    return both.astype(jnp.float32) * unit


def body(
    nx, nz, ny, share,
    doc_pick, word_pick, live, counts_hbm, doc_hbm, word_hbm, mass_hbm, noise_hbm,
    doc_out, word_out,
    slot_vm, slot_ref, cbuf, dbuf, word_ref, mass_ref, noise_ref,
    cnt, cnt_sib, cnt_t, prob, gall, gam, part, part_go, got, hits, hits_go, got_x, sum_go, got_z,
    tot_y, tot_c, tot_x, tot_z,
    in_sem, doc_sem, cnt_sem,
    pz_s, pz_r, px_s, px_r, pc_s, pc_r,
    s_s, s_r, g_s, g_r, gc_s, gc_r,
    hx_s, hx_r, hz_s, hz_r,
    ty_s, ty_r, tc_s, tc_r, tx_s, tx_r, tz_s, tz_r,
):
    slots, block = counts_hbm.shape[2], counts_hbm.shape[3]
    panel, topics = prob.shape[1], prob.shape[2]
    wblocks = panel // block
    rows_x = nz * share
    sub = share // CHAINS
    docs = ny * sub
    dp = lax.axis_index("dp")
    vo = lax.axis_index("vocab")
    x, z = dp // nz, lax.rem(dp, nz)
    y, c = vo // 2, lax.rem(vo, 2)
    sib = 1 - c

    def at_y(j):
        return (dp, lax.rem(y + j, ny) * 2 + c)

    def at_x(j):
        return (lax.rem(x + j, nx) * nz + z, vo)

    def at_z(j):
        return (x * nz + lax.rem(z + j, nz), vo)

    at_c = (dp, y * 2 + sib)

    def remote(src, dst, s, r, to):
        return pltpu.make_async_remote_copy(
            src_ref=src, dst_ref=dst, send_sem=s, recv_sem=r, device_id=to, device_id_type=MESH
        )

    word_in = pltpu.make_async_copy(word_hbm, word_ref, in_sem.at[0])
    mass_in = pltpu.make_async_copy(mass_hbm, mass_ref, in_sem.at[1])
    word_in.start()
    mass_in.start()

    barrier = pltpu.get_barrier_semaphore()
    peers = [at_y(j) for j in range(1, ny)] + [at_c]
    peers += [at_x(j) for j in range(1, nx)] + [at_z(j) for j in range(1, nz)]
    for to in peers:
        pl.semaphore_signal(barrier, inc=1, device_id=to, device_id_type=MESH)

    counts_in = pltpu.make_async_copy(counts_hbm.at[0, 0], cbuf.at[pl.ds(0, slots)], in_sem.at[2])
    counts_in.start()
    doc_in = [
        pltpu.make_async_copy(
            doc_hbm.at[pl.ds((2 * q + c) * share, share)], dbuf.at[q], doc_sem.at[q]
        )
        for q in range(ny)
    ]
    for copy in doc_in:
        copy.start()
    noise_in = pltpu.make_async_copy(noise_hbm, noise_ref, in_sem.at[3])
    noise_in.start()

    lane = lax.broadcasted_iota(jnp.int32, (1, 128), 1)
    slot_of = jnp.full((1, 128), slots, jnp.int32)
    for s in range(slots):
        key = doc_pick[0, 0, s] * wblocks + word_pick[0, 0, s]
        use = jnp.where(s < live[0, 0], s, slots)
        slot_of = jnp.where(lane == key, use, slot_of)
    slot_vm[...] = slot_of
    slot_in = pltpu.make_async_copy(slot_vm, slot_ref, in_sem.at[4])
    slot_in.start()

    def word_rows(jx, jz):
        row = (lax.rem(x - jx + nx, nx) * nz + lax.rem(z - jz + nz, nz)) * share
        return pl.ds(pl.multiple_of(row, share), share)

    def word_block(jx):
        return pl.ds(pl.multiple_of(lax.rem(x - jx + nx, nx) * rows_x, rows_x), rows_x)

    def shard(jx, jz):
        return prob.at[c, word_rows(jx, jz)]

    word_in.wait()
    mass_in.wait()
    prob[c, word_rows(0, 0), :] = (word_ref[...] / mass_ref[...]).astype(jnp.bfloat16)
    pl.semaphore_wait(barrier, len(peers))

    pz = {j: remote(shard(0, 0), shard(0, 0), pz_s.at[j], pz_r.at[j], at_z(j)) for j in range(1, nz)}
    px = {
        (jx, jz): remote(shard(0, jz), shard(0, jz), px_s.at[jx, jz], px_r.at[jx, jz], at_x(jx))
        for jx in range(1, nx)
        for jz in range(nz)
    }
    pc = [
        remote(prob.at[c, word_block(jx)], prob.at[c, word_block(jx)], pc_s.at[jx], pc_r.at[jx], at_c)
        for jx in range(nx)
    ]
    for j in near_first(nz):
        pz[j].start()
    for jx in far_first(nx):
        px[jx, 0].start()

    for copy in doc_in:
        copy.wait()
    for h in range(CHAINS):
        for q in range(ny):
            gall[q, c, h] = dbuf[q, h * sub:(h + 1) * sub, :].astype(jnp.bfloat16)
        gam[h] = dbuf[y, h * sub:(h + 1) * sub, :]

    for jz in near_first(nz):
        remote(shard(0, jz), shard(0, jz), pz_s.at[jz], pz_r.at[jz], at_z(jz)).wait_recv()
        for jx in far_first(nx):
            px[jx, jz].start()
    pc[0].start()

    counts_in.wait()
    slot_in.wait()
    cbuf[slots] = jnp.zeros((block, block), jnp.int32)
    pairs = block // share // 2

    def place(t, _):
        d, w = t // wblocks, lax.rem(t, wblocks)
        slot = slot_ref[0, t]
        col = pl.ds(pl.multiple_of(w * block, block), block)
        for k in range(pairs):
            for other in range(2):
                core = sib if other else c
                piece = cbuf[slot, pl.ds(pl.multiple_of((2 * k + core) * share, share), share), :]
                piece = piece.astype(jnp.float32).astype(jnp.bfloat16)
                for h in range(CHAINS):
                    row = pl.ds(pl.multiple_of((d * pairs + k) * sub, sub), sub)
                    val = piece[h * sub:(h + 1) * sub]
                    if other:
                        cnt_sib[h, row, col] = val
                    else:
                        cnt[c, h, row, col] = val
        return 0

    lax.fori_loop(0, slots, place, 0)
    cnt_go = remote(cnt_sib, cnt.at[c], cnt_sem.at[0], cnt_sem.at[1], at_c)
    cnt_go.start()

    def turn(w, _):
        row = pl.ds(pl.multiple_of(w * block, block), block)
        for d in range(slots // wblocks):
            tile = cbuf[slot_ref[0, d * wblocks + w]].astype(jnp.float32)
            cnt_t[row, d * block:(d + 1) * block] = tile.T.astype(jnp.bfloat16)
        return 0

    lax.fori_loop(0, wblocks, turn, 0)

    def chain_gamma(h):
        return jnp.concatenate([gall[q, c, h] for q in range(ny)], axis=0)

    both = jnp.concatenate([chain_gamma(h) for h in range(CHAINS)], axis=0)

    def first_sums(side, jx, first):
        words = word_block(jx)
        p = prob[side, words, :]
        n = jnp.concatenate([cnt[side, h, :, words] for h in range(CHAINS)], axis=0)
        ratios = (n.astype(jnp.float32) / nt_dot(both, p)).astype(jnp.bfloat16)
        add = jnp.dot(ratios, p, preferred_element_type=jnp.float32)
        for h in range(CHAINS):
            if first:
                part[h] = add[h * docs:(h + 1) * docs]
            else:
                part[h] += add[h * docs:(h + 1) * docs]

    def sib_sums(jx):
        theirs = prob.at[sib, word_block(jx)]
        remote(theirs, theirs, pc_s.at[jx], pc_r.at[jx], at_c).wait_recv()
        first_sums(sib, jx, False)

    first_sums(c, 0, True)
    remote(cnt_sib, cnt.at[sib], cnt_sem.at[0], cnt_sem.at[1], at_c).wait_recv()
    sib_sums(0)
    before = None
    for jx in near_first(nx):
        for jz in [0] + near_first(nz):
            remote(shard(jx, jz), shard(jx, jz), px_s.at[jx, jz], px_r.at[jx, jz], at_x(jx)).wait_recv()
        pc[jx].start()
        first_sums(c, jx, False)
        if before is not None:
            sib_sums(before)
        before = jx
    sib_sums(before)

    chunk = min(512, panel)

    def partial_sums(h):
        g = chain_gamma(h)
        total = None
        for side in range(2):
            for k in range(panel // chunk):
                words = pl.ds(k * chunk, chunk)
                p = prob[side, words, :]
                n = cnt[side, h, :, words].astype(jnp.float32)
                ratios = (n / nt_dot(g, p)).astype(jnp.bfloat16)
                add = jnp.dot(ratios, p, preferred_element_type=jnp.float32)
                total = add if total is None else total + add
        part[h] = total

    def doc_rows(j):
        return pl.ds(pl.multiple_of(lax.rem(y + j + ny, ny) * sub, sub), sub)

    def send_sums(h, j):
        to = lax.rem(y + j, ny)
        return remote(part_go.at[h, to], got.at[h, j], s_s.at[h, j], s_r.at[h, j], at_y(j))

    def pack_sums(h):
        for q in range(ny):
            rows = slice(q * sub, (q + 1) * sub)
            store_packed(part_go.at[h, q], part[h, rows, :] * gall[q, c, h].astype(jnp.float32))

    def send_gamma(h, j):
        own = gall.at[y, c, h]
        return remote(own, own, g_s.at[h, j], g_r.at[h, j], at_y(j))

    def wait_gamma(h, j):
        theirs = gall.at[lax.rem(y - j + ny, ny), c, h]
        remote(theirs, theirs, g_s.at[h, j], g_r.at[h, j], at_y(j)).wait_recv()

    for it in range(ITERS):
        for h in range(CHAINS):
            if it:
                for j in near_first(ny):
                    wait_gamma(h, j)
                for j in range(1, ny):
                    send_sums(h, j).wait_send()
                partial_sums(h)
            pack_sums(h)
            for j in far_first(ny):
                send_sums(h, j).start()
        for h in range(CHAINS):
            total = None
            for j in near_first(ny):
                send_sums(h, j).wait_recv()
                add = unpack(got.at[h, j])
                total = add if total is None else total + add
            total = part[h, doc_rows(0), :] + total / gall[y, c, h].astype(jnp.float32)
            gam[h] = ALPHA_PRIOR + gam[h] * total
            if it:
                for j in range(1, ny):
                    send_gamma(h, j).wait_send()
            gall[y, c, h] = gam[h].astype(jnp.bfloat16)
            for j in far_first(ny):
                send_gamma(h, j).start()

    final = jnp.concatenate([gam[h] for h in range(CHAINS)], axis=0)
    tot_y[0] = jnp.sum(final - ALPHA_PRIOR, axis=0, keepdims=True)

    def send_ty(j):
        return remote(tot_y.at[0], tot_y.at[j], ty_s.at[j], ty_r.at[j], at_y(j))

    for j in far_first(ny):
        send_ty(j).start()
    doc_out[...] = final / (jnp.sum(final, axis=1, keepdims=True) / topics)

    def give(h):
        mine = gall.at[:, c, h]
        return remote(mine, mine, gc_s.at[h], gc_r.at[h], at_c)

    def wait_give(h):
        theirs = gall.at[:, sib, h]
        remote(theirs, theirs, gc_s.at[h], gc_r.at[h], at_c).wait_recv()

    for h in range(CHAINS):
        for j in near_first(ny):
            wait_gamma(h, j)
        give(h).start()
    total = tot_y[0]
    for j in near_first(ny):
        send_ty(j).wait_recv()
        total = total + tot_y[j]
    tot_c[0] = total
    send_tc = remote(tot_c.at[0], tot_c.at[1], tc_s, tc_r, at_c)
    send_tc.start()
    for h in range(CHAINS):
        wait_give(h)

    def z_rows(j):
        return pl.ds(pl.multiple_of(lax.rem(z + j, nz) * share, share), share)

    def send_hx(jx, jz):
        return remote(
            hits_go.at[jx, lax.rem(z + jz, nz)], got_x.at[jx, jz],
            hx_s.at[jx, jz], hx_r.at[jx, jz], at_x(jx),
        )

    def send_hz(j):
        return remote(sum_go.at[j], got_z.at[j], hz_s.at[j], hz_r.at[j], at_z(j))

    def send_tx(j):
        return remote(tot_x.at[0], tot_x.at[j], tx_s.at[j], tx_r.at[j], at_x(j))

    def send_tz(j):
        return remote(tot_z.at[0], tot_z.at[j], tz_s.at[j], tz_r.at[j], at_z(j))

    gamma_all = gall[...].reshape(2 * CHAINS * docs, topics)
    z_order = far_first(nz) + [0]
    for jx in far_first(nx) + [0]:
        words = word_block(nx - jx)
        p = prob[c, words, :]
        ratios = (cnt_t[words, :].astype(jnp.float32) / nt_dot(p, gamma_all)).astype(jnp.bfloat16)
        found = jnp.dot(ratios, gamma_all, preferred_element_type=jnp.float32) * p.astype(jnp.float32)
        if not jx:
            hits[...] = found
        else:
            for q in range(nz):
                store_packed(hits_go.at[jx, q], found[q * share:(q + 1) * share])
            for jz in z_order:
                send_hx(jx, jz).start()

    send_tc.wait_recv()
    tot_x[0] = tot_c[0] + tot_c[1]
    for j in far_first(nx):
        send_tx(j).start()
    total = tot_x[0]
    for j in near_first(nx):
        send_tx(j).wait_recv()
        total = total + tot_x[j]
    tot_z[0] = total
    for j in far_first(nz):
        send_tz(j).start()

    for jz in z_order:
        total = hits[z_rows(jz), :]
        for jx in range(1, nx):
            send_hx(jx, jz).wait_recv()
            total = total + unpack(got_x.at[jx, jz])
        if jz:
            store_packed(sum_go.at[jz], total)
            send_hz(jz).start()
    reduced = total

    totals = tot_z[0]
    for j in near_first(nz):
        send_tz(j).wait_recv()
        totals = totals + tot_z[j]
    noise_in.wait()
    for j in near_first(nz):
        send_hz(j).wait_recv()
        reduced = reduced + unpack(got_z.at[j])
    word = word_ref[...]
    probs = word / mass_ref[...]
    counted = reduced * (probs / prob[c, word_rows(0, 0), :].astype(jnp.float32))
    drift = BETA_PRIOR - word + GRAD_SCALE * (counted - totals * probs)
    word_out[...] = jnp.abs(word + HALF_STEP * drift + jnp.sqrt(word) * noise_ref[...])

    for j in range(1, nz):
        pz[j].wait_send()
        send_hz(j).wait_send()
        send_tz(j).wait_send()
    for jx in range(1, nx):
        send_tx(jx).wait_send()
        for jz in range(nz):
            px[jx, jz].wait_send()
            send_hx(jx, jz).wait_send()
    for jx in range(nx):
        pc[jx].wait_send()
    cnt_go.wait_send()
    send_tc.wait_send()
    for h in range(CHAINS):
        give(h).wait_send()
        for j in range(1, ny):
            send_sums(h, j).wait_send()
            send_gamma(h, j).wait_send()
    for j in range(1, ny):
        send_ty(j).wait_send()


def shards(counts, tile_doc, tile_word, tile_live, doc_init, topic_word, topic_mass, noise):
    topics = topic_mass.shape[0]
    slots, block = counts.shape[2], counts.shape[3]
    n_dp, n_vocab = lax.axis_size("dp"), lax.axis_size("vocab")
    nx = X_CHIPS
    nz, ny = n_dp // nx, n_vocab // 2
    share = topic_word.shape[0]
    panel = share * n_dp
    sub = share // CHAINS
    docs = ny * sub

    f32, bf16, i32, dma = jnp.float32, jnp.bfloat16, jnp.int32, pltpu.SemaphoreType.DMA
    vmem = pl.BlockSpec(memory_space=pltpu.VMEM)
    smem = pl.BlockSpec(memory_space=pltpu.SMEM)
    hbm = pl.BlockSpec(memory_space=pl.ANY)
    return pl.pallas_call(
        functools.partial(body, nx, nz, ny, share),
        out_shape=(
            jax.ShapeDtypeStruct((share, topics), f32),
            jax.ShapeDtypeStruct((share, topics), f32),
        ),
        in_specs=[smem, smem, smem, hbm, hbm, hbm, hbm, hbm],
        out_specs=(vmem, vmem),
        scratch_shapes=[
            pltpu.VMEM((1, 128), jnp.int32),
            pltpu.SMEM((1, 128), jnp.int32),
            pltpu.VMEM((slots + 1, block, block), jnp.int32),
            pltpu.VMEM((ny, share, topics), f32),
            pltpu.VMEM((share, topics), f32),
            pltpu.VMEM((1, topics), f32),
            pltpu.VMEM((share, topics), f32),
            pltpu.VMEM((2, CHAINS, docs, panel), bf16),
            pltpu.VMEM((CHAINS, docs, panel), bf16),
            pltpu.VMEM((panel, 2 * CHAINS * docs), bf16),
            pltpu.VMEM((2, panel, topics), bf16),
            pltpu.VMEM((ny, 2, CHAINS, sub, topics), bf16),
            pltpu.VMEM((CHAINS, sub, topics), f32),
            pltpu.VMEM((CHAINS, docs, topics), f32),
            pltpu.VMEM((CHAINS, ny, sub // 2 + 1, topics), i32),
            pltpu.VMEM((CHAINS, ny, sub // 2 + 1, topics), i32),
            pltpu.VMEM((nz * share, topics), f32),
            pltpu.VMEM((nx, nz, share // 2 + 1, topics), i32),
            pltpu.VMEM((nx, nz, share // 2 + 1, topics), i32),
            pltpu.VMEM((nz, share // 2 + 1, topics), i32),
            pltpu.VMEM((nz, share // 2 + 1, topics), i32),
            pltpu.VMEM((ny, 1, topics), f32),
            pltpu.VMEM((2, 1, topics), f32),
            pltpu.VMEM((nx, 1, topics), f32),
            pltpu.VMEM((nz, 1, topics), f32),
            dma((5,)), dma((ny,)), dma((2,)),
            dma((nz,)), dma((nz,)), dma((nx, nz)), dma((nx, nz)), dma((nx,)), dma((nx,)),
            dma((CHAINS, ny)), dma((CHAINS, ny)), dma((CHAINS, ny)), dma((CHAINS, ny)),
            dma((CHAINS,)), dma((CHAINS,)),
            dma((nx, nz)), dma((nx, nz)), dma((nz,)), dma((nz,)),
            dma((ny,)), dma((ny,)), dma, dma, dma((nx,)), dma((nx,)), dma((nz,)), dma((nz,)),
        ],
        compiler_params=pltpu.CompilerParams(
            collective_id=0, has_side_effects=True, vmem_limit_bytes=VMEM_LIMIT
        ),
    )(tile_doc, tile_word, tile_live, counts, doc_init, topic_word, topic_mass[None, :], noise)


def solution(mesh):
    return jax.shard_map(
        shards,
        mesh=mesh,
        in_specs=(
            P("dp", "vocab", None, None, None),
            P("dp", "vocab", None),
            P("dp", "vocab", None),
            P("dp", "vocab"),
            P("dp", None),
            P(("vocab", "dp"), None),
            P(),
            P(("vocab", "dp"), None),
        ),
        out_specs=(P(("dp", "vocab"), None), P(("vocab", "dp"), None)),
        check_vma=False,
    )
```

```python
import functools

import jax
import jax.numpy as jnp
from jax import lax
from jax.experimental import pallas as pl
from jax.experimental.pallas import tpu as pltpu
from jax.sharding import PartitionSpec as P

ITERS = 3
ALPHA_PRIOR = 0.1
BETA_PRIOR = 0.01
HALF_STEP = 0.05
GRAD_SCALE = 16.0
MESH = pl.DeviceIdType.MESH
CHAINS = 2
CODES = 65535.0
SCALE_STEPS = 1024.0
X_CHIPS = 4
VMEM_LIMIT = 58 * 2**20


def far_first(count):
    return sorted(range(1, count), key=lambda j: -min(j, count - j))


def near_first(count):
    return sorted(range(1, count), key=lambda j: min(j, count - j))


def nt_dot(a, b):
    return lax.dot_general(a, b, (((1,), (1,)), ((), ())), preferred_element_type=jnp.float32)


def pack(values):
    half = values.shape[0] // 2
    top = jnp.maximum(jnp.max(values, axis=0, keepdims=True), 1e-30)
    scale = (jnp.log2(top) * SCALE_STEPS + 1.0).astype(jnp.int32)
    factor = jnp.exp2(scale.astype(jnp.float32) * (-1.0 / SCALE_STEPS)) * CODES
    code = jnp.minimum(values * factor + 0.5, CODES).astype(jnp.int32)
    return code[:half] | (code[half:] << 16), scale


def store_packed(ref, scale_ref, values):
    ref[...], scale_ref[...] = pack(values)


def unpack(ref, scale_ref):
    code = ref[...]
    unit = jnp.exp2(scale_ref[...].astype(jnp.float32) * (1.0 / SCALE_STEPS)) * (1.0 / CODES)
    both = jnp.concatenate([code & 0xFFFF, (code >> 16) & 0xFFFF], axis=0)
    return both.astype(jnp.float32) * unit


def body(
    nx, nz, ny, share,
    doc_pick, word_pick, live, counts_hbm, doc_hbm, word_hbm, mass_hbm, noise_hbm,
    doc_out, word_out,
    slot_vm, slot_ref, cbuf, dbuf, word_ref, mass_ref, noise_ref,
    cnt, cnt_sib, cnt_t, prob, gall, gam, part, part_go, part_sc, got, got_sc,
    hits, hits_go, hits_sc, got_x, got_xs, sum_go, sum_sc, got_z, got_zs,
    tot_y, tot_c, tot_x, tot_z,
    in_sem, doc_sem, cnt_sem,
    pz_s, pz_r, px_s, px_r, pc_s, pc_r,
    s_s, s_r, sc_s, sc_r, g_s, g_r, gc_s, gc_r,
    hx_s, hx_r, xs_s, xs_r, hz_s, hz_r, zs_s, zs_r,
    ty_s, ty_r, tc_s, tc_r, tx_s, tx_r, tz_s, tz_r,
):
    slots, block = counts_hbm.shape[2], counts_hbm.shape[3]
    panel, topics = prob.shape[1], prob.shape[2]
    wblocks = panel // block
    rows_x = nz * share
    sub = share // CHAINS
    docs = ny * sub
    dp = lax.axis_index("dp")
    vo = lax.axis_index("vocab")
    x, z = dp // nz, lax.rem(dp, nz)
    y, c = vo // 2, lax.rem(vo, 2)
    sib = 1 - c

    def at_y(j):
        return (dp, lax.rem(y + j, ny) * 2 + c)

    def at_x(j):
        return (lax.rem(x + j, nx) * nz + z, vo)

    def at_z(j):
        return (x * nz + lax.rem(z + j, nz), vo)

    at_c = (dp, y * 2 + sib)

    def remote(src, dst, s, r, to):
        return pltpu.make_async_remote_copy(
            src_ref=src, dst_ref=dst, send_sem=s, recv_sem=r, device_id=to, device_id_type=MESH
        )

    word_in = pltpu.make_async_copy(word_hbm, word_ref, in_sem.at[0])
    mass_in = pltpu.make_async_copy(mass_hbm, mass_ref, in_sem.at[1])
    word_in.start()
    mass_in.start()

    barrier = pltpu.get_barrier_semaphore()
    peers = [at_y(j) for j in range(1, ny)] + [at_c]
    peers += [at_x(j) for j in range(1, nx)] + [at_z(j) for j in range(1, nz)]
    for to in peers:
        pl.semaphore_signal(barrier, inc=1, device_id=to, device_id_type=MESH)

    counts_in = pltpu.make_async_copy(counts_hbm.at[0, 0], cbuf.at[pl.ds(0, slots)], in_sem.at[2])
    counts_in.start()
    doc_in = [
        pltpu.make_async_copy(
            doc_hbm.at[pl.ds((2 * q + c) * share, share)], dbuf.at[q], doc_sem.at[q]
        )
        for q in range(ny)
    ]
    for copy in doc_in:
        copy.start()
    noise_in = pltpu.make_async_copy(noise_hbm, noise_ref, in_sem.at[3])
    noise_in.start()

    lane = lax.broadcasted_iota(jnp.int32, (1, 128), 1)
    slot_of = jnp.full((1, 128), slots, jnp.int32)
    for s in range(slots):
        key = doc_pick[0, 0, s] * wblocks + word_pick[0, 0, s]
        use = jnp.where(s < live[0, 0], s, slots)
        slot_of = jnp.where(lane == key, use, slot_of)
    slot_vm[...] = slot_of
    slot_in = pltpu.make_async_copy(slot_vm, slot_ref, in_sem.at[4])
    slot_in.start()

    def word_rows(jx, jz):
        row = (lax.rem(x - jx + nx, nx) * nz + lax.rem(z - jz + nz, nz)) * share
        return pl.ds(pl.multiple_of(row, share), share)

    def word_block(jx):
        return pl.ds(pl.multiple_of(lax.rem(x - jx + nx, nx) * rows_x, rows_x), rows_x)

    def shard(jx, jz):
        return prob.at[c, word_rows(jx, jz)]

    word_in.wait()
    mass_in.wait()
    prob[c, word_rows(0, 0), :] = (word_ref[...] / mass_ref[...]).astype(jnp.bfloat16)
    pl.semaphore_wait(barrier, len(peers))

    pz = {j: remote(shard(0, 0), shard(0, 0), pz_s.at[j], pz_r.at[j], at_z(j)) for j in range(1, nz)}
    px = {
        (jx, jz): remote(shard(0, jz), shard(0, jz), px_s.at[jx, jz], px_r.at[jx, jz], at_x(jx))
        for jx in range(1, nx)
        for jz in range(nz)
    }
    pc = [
        remote(prob.at[c, word_block(jx)], prob.at[c, word_block(jx)], pc_s.at[jx], pc_r.at[jx], at_c)
        for jx in range(nx)
    ]
    for j in near_first(nz):
        pz[j].start()
    for jx in far_first(nx):
        px[jx, 0].start()

    for copy in doc_in:
        copy.wait()
    for h in range(CHAINS):
        for q in range(ny):
            gall[q, c, h] = dbuf[q, h * sub:(h + 1) * sub, :].astype(jnp.bfloat16)
        gam[h] = dbuf[y, h * sub:(h + 1) * sub, :]

    for jz in near_first(nz):
        remote(shard(0, jz), shard(0, jz), pz_s.at[jz], pz_r.at[jz], at_z(jz)).wait_recv()
        for jx in far_first(nx):
            px[jx, jz].start()
    pc[0].start()

    counts_in.wait()
    slot_in.wait()
    cbuf[slots] = jnp.zeros((block, block), jnp.int32)
    pairs = block // share // 2

    def place(t, _):
        d, w = t // wblocks, lax.rem(t, wblocks)
        slot = slot_ref[0, t]
        col = pl.ds(pl.multiple_of(w * block, block), block)
        for k in range(pairs):
            for other in range(2):
                core = sib if other else c
                piece = cbuf[slot, pl.ds(pl.multiple_of((2 * k + core) * share, share), share), :]
                piece = piece.astype(jnp.float32).astype(jnp.bfloat16)
                for h in range(CHAINS):
                    row = pl.ds(pl.multiple_of((d * pairs + k) * sub, sub), sub)
                    val = piece[h * sub:(h + 1) * sub]
                    if other:
                        cnt_sib[h, row, col] = val
                    else:
                        cnt[c, h, row, col] = val
        return 0

    lax.fori_loop(0, slots, place, 0)
    cnt_go = remote(cnt_sib, cnt.at[c], cnt_sem.at[0], cnt_sem.at[1], at_c)
    cnt_go.start()

    def turn(w, _):
        row = pl.ds(pl.multiple_of(w * block, block), block)
        for d in range(slots // wblocks):
            tile = cbuf[slot_ref[0, d * wblocks + w]].astype(jnp.float32)
            cnt_t[row, d * block:(d + 1) * block] = tile.T.astype(jnp.bfloat16)
        return 0

    lax.fori_loop(0, wblocks, turn, 0)

    def chain_gamma(h):
        return jnp.concatenate([gall[q, c, h] for q in range(ny)], axis=0)

    both = jnp.concatenate([chain_gamma(h) for h in range(CHAINS)], axis=0)

    def first_sums(side, jx, first):
        words = word_block(jx)
        p = prob[side, words, :]
        n = jnp.concatenate([cnt[side, h, :, words] for h in range(CHAINS)], axis=0)
        ratios = (n.astype(jnp.float32) / nt_dot(both, p)).astype(jnp.bfloat16)
        add = jnp.dot(ratios, p, preferred_element_type=jnp.float32)
        for h in range(CHAINS):
            if first:
                part[h] = add[h * docs:(h + 1) * docs]
            else:
                part[h] += add[h * docs:(h + 1) * docs]

    def sib_sums(jx):
        theirs = prob.at[sib, word_block(jx)]
        remote(theirs, theirs, pc_s.at[jx], pc_r.at[jx], at_c).wait_recv()
        first_sums(sib, jx, False)

    first_sums(c, 0, True)
    remote(cnt_sib, cnt.at[sib], cnt_sem.at[0], cnt_sem.at[1], at_c).wait_recv()
    sib_sums(0)
    before = None
    for jx in near_first(nx):
        for jz in [0] + near_first(nz):
            remote(shard(jx, jz), shard(jx, jz), px_s.at[jx, jz], px_r.at[jx, jz], at_x(jx)).wait_recv()
        pc[jx].start()
        first_sums(c, jx, False)
        if before is not None:
            sib_sums(before)
        before = jx
    sib_sums(before)

    chunk = min(512, panel)

    def partial_sums(h):
        g = chain_gamma(h)
        total = None
        for side in range(2):
            for k in range(panel // chunk):
                words = pl.ds(k * chunk, chunk)
                p = prob[side, words, :]
                n = cnt[side, h, :, words].astype(jnp.float32)
                ratios = (n / nt_dot(g, p)).astype(jnp.bfloat16)
                add = jnp.dot(ratios, p, preferred_element_type=jnp.float32)
                total = add if total is None else total + add
        part[h] = total

    def doc_rows(j):
        return pl.ds(pl.multiple_of(lax.rem(y + j + ny, ny) * sub, sub), sub)

    def send_sums(h, j):
        to = lax.rem(y + j, ny)
        return remote(part_go.at[h, to], got.at[h, j], s_s.at[h, j], s_r.at[h, j], at_y(j))

    def send_scale(h, j):
        to = lax.rem(y + j, ny)
        return remote(part_sc.at[h, to], got_sc.at[h, j], sc_s.at[h, j], sc_r.at[h, j], at_y(j))

    def pack_sums(h):
        for q in range(ny):
            rows = slice(q * sub, (q + 1) * sub)
            here = part[h, rows, :] * gall[q, c, h].astype(jnp.float32)
            store_packed(part_go.at[h, q], part_sc.at[h, q], here)

    def send_gamma(h, j):
        own = gall.at[y, c, h]
        return remote(own, own, g_s.at[h, j], g_r.at[h, j], at_y(j))

    def wait_gamma(h, j):
        theirs = gall.at[lax.rem(y - j + ny, ny), c, h]
        remote(theirs, theirs, g_s.at[h, j], g_r.at[h, j], at_y(j)).wait_recv()

    for it in range(ITERS):
        for h in range(CHAINS):
            if it:
                for j in near_first(ny):
                    wait_gamma(h, j)
                for j in range(1, ny):
                    send_sums(h, j).wait_send()
                    send_scale(h, j).wait_send()
                partial_sums(h)
            pack_sums(h)
            for j in far_first(ny):
                send_scale(h, j).start()
                send_sums(h, j).start()
        for h in range(CHAINS):
            total = None
            for j in near_first(ny):
                send_scale(h, j).wait_recv()
                send_sums(h, j).wait_recv()
                add = unpack(got.at[h, j], got_sc.at[h, j])
                total = add if total is None else total + add
            total = part[h, doc_rows(0), :] + total / gall[y, c, h].astype(jnp.float32)
            gam[h] = ALPHA_PRIOR + gam[h] * total
            if it:
                for j in range(1, ny):
                    send_gamma(h, j).wait_send()
            gall[y, c, h] = gam[h].astype(jnp.bfloat16)
            for j in far_first(ny):
                send_gamma(h, j).start()

    final = jnp.concatenate([gam[h] for h in range(CHAINS)], axis=0)
    tot_y[0] = jnp.sum(final - ALPHA_PRIOR, axis=0, keepdims=True)

    def send_ty(j):
        return remote(tot_y.at[0], tot_y.at[j], ty_s.at[j], ty_r.at[j], at_y(j))

    for j in far_first(ny):
        send_ty(j).start()
    doc_out[...] = final / (jnp.sum(final, axis=1, keepdims=True) / topics)

    def give(h):
        mine = gall.at[:, c, h]
        return remote(mine, mine, gc_s.at[h], gc_r.at[h], at_c)

    def wait_give(h):
        theirs = gall.at[:, sib, h]
        remote(theirs, theirs, gc_s.at[h], gc_r.at[h], at_c).wait_recv()

    for h in range(CHAINS):
        for j in near_first(ny):
            wait_gamma(h, j)
        give(h).start()
    total = tot_y[0]
    for j in near_first(ny):
        send_ty(j).wait_recv()
        total = total + tot_y[j]
    tot_c[0] = total
    send_tc = remote(tot_c.at[0], tot_c.at[1], tc_s, tc_r, at_c)
    send_tc.start()
    for h in range(CHAINS):
        wait_give(h)

    def z_rows(j):
        return pl.ds(pl.multiple_of(lax.rem(z + j, nz) * share, share), share)

    def send_hx(jx, jz):
        return remote(
            hits_go.at[jx, lax.rem(z + jz, nz)], got_x.at[jx, jz],
            hx_s.at[jx, jz], hx_r.at[jx, jz], at_x(jx),
        )

    def send_xs(jx):
        return remote(hits_sc.at[jx], got_xs.at[jx], xs_s.at[jx], xs_r.at[jx], at_x(jx))

    def send_zs(j):
        return remote(sum_sc.at[j], got_zs.at[j], zs_s.at[j], zs_r.at[j], at_z(j))

    def send_hz(j):
        return remote(sum_go.at[j], got_z.at[j], hz_s.at[j], hz_r.at[j], at_z(j))

    def send_tx(j):
        return remote(tot_x.at[0], tot_x.at[j], tx_s.at[j], tx_r.at[j], at_x(j))

    def send_tz(j):
        return remote(tot_z.at[0], tot_z.at[j], tz_s.at[j], tz_r.at[j], at_z(j))

    gamma_all = gall[...].reshape(2 * CHAINS * docs, topics)
    z_order = far_first(nz) + [0]
    for jx in far_first(nx) + [0]:
        words = word_block(nx - jx)
        p = prob[c, words, :]
        ratios = (cnt_t[words, :].astype(jnp.float32) / nt_dot(p, gamma_all)).astype(jnp.bfloat16)
        found = jnp.dot(ratios, gamma_all, preferred_element_type=jnp.float32) * p.astype(jnp.float32)
        if not jx:
            hits[...] = found
        else:
            for q in range(nz):
                store_packed(hits_go.at[jx, q], hits_sc.at[jx, q], found[q * share:(q + 1) * share])
            send_xs(jx).start()
            for jz in z_order:
                send_hx(jx, jz).start()

    send_tc.wait_recv()
    tot_x[0] = tot_c[0] + tot_c[1]
    for j in far_first(nx):
        send_tx(j).start()
    total = tot_x[0]
    for j in near_first(nx):
        send_tx(j).wait_recv()
        total = total + tot_x[j]
    tot_z[0] = total
    for j in far_first(nz):
        send_tz(j).start()

    for jx in far_first(nx):
        send_xs(jx).wait_recv()
    for jz in z_order:
        total = hits[z_rows(jz), :]
        for jx in range(1, nx):
            send_hx(jx, jz).wait_recv()
            total = total + unpack(got_x.at[jx, jz], got_xs.at[jx, lax.rem(z + jz, nz)])
        if jz:
            store_packed(sum_go.at[jz], sum_sc.at[jz], total)
            send_zs(jz).start()
            send_hz(jz).start()
    reduced = total

    totals = tot_z[0]
    for j in near_first(nz):
        send_tz(j).wait_recv()
        totals = totals + tot_z[j]
    noise_in.wait()
    for j in near_first(nz):
        send_zs(j).wait_recv()
        send_hz(j).wait_recv()
        reduced = reduced + unpack(got_z.at[j], got_zs.at[j])
    word = word_ref[...]
    probs = word / mass_ref[...]
    counted = reduced * (probs / prob[c, word_rows(0, 0), :].astype(jnp.float32))
    drift = BETA_PRIOR - word + GRAD_SCALE * (counted - totals * probs)
    word_out[...] = jnp.abs(word + HALF_STEP * drift + jnp.sqrt(word) * noise_ref[...])

    for j in range(1, nz):
        pz[j].wait_send()
        send_hz(j).wait_send()
        send_zs(j).wait_send()
        send_tz(j).wait_send()
    for jx in range(1, nx):
        send_tx(jx).wait_send()
        send_xs(jx).wait_send()
        for jz in range(nz):
            px[jx, jz].wait_send()
            send_hx(jx, jz).wait_send()
    for jx in range(nx):
        pc[jx].wait_send()
    cnt_go.wait_send()
    send_tc.wait_send()
    for h in range(CHAINS):
        give(h).wait_send()
        for j in range(1, ny):
            send_sums(h, j).wait_send()
            send_scale(h, j).wait_send()
            send_gamma(h, j).wait_send()
    for j in range(1, ny):
        send_ty(j).wait_send()


def shards(counts, tile_doc, tile_word, tile_live, doc_init, topic_word, topic_mass, noise):
    topics = topic_mass.shape[0]
    slots, block = counts.shape[2], counts.shape[3]
    n_dp, n_vocab = lax.axis_size("dp"), lax.axis_size("vocab")
    nx = X_CHIPS
    nz, ny = n_dp // nx, n_vocab // 2
    share = topic_word.shape[0]
    panel = share * n_dp
    sub = share // CHAINS
    docs = ny * sub

    f32, bf16, i32, dma = jnp.float32, jnp.bfloat16, jnp.int32, pltpu.SemaphoreType.DMA
    vmem = pl.BlockSpec(memory_space=pltpu.VMEM)
    smem = pl.BlockSpec(memory_space=pltpu.SMEM)
    hbm = pl.BlockSpec(memory_space=pl.ANY)
    return pl.pallas_call(
        functools.partial(body, nx, nz, ny, share),
        out_shape=(
            jax.ShapeDtypeStruct((share, topics), f32),
            jax.ShapeDtypeStruct((share, topics), f32),
        ),
        in_specs=[smem, smem, smem, hbm, hbm, hbm, hbm, hbm],
        out_specs=(vmem, vmem),
        scratch_shapes=[
            pltpu.VMEM((1, 128), jnp.int32),
            pltpu.SMEM((1, 128), jnp.int32),
            pltpu.VMEM((slots + 1, block, block), jnp.int32),
            pltpu.VMEM((ny, share, topics), f32),
            pltpu.VMEM((share, topics), f32),
            pltpu.VMEM((1, topics), f32),
            pltpu.VMEM((share, topics), f32),
            pltpu.VMEM((2, CHAINS, docs, panel), bf16),
            pltpu.VMEM((CHAINS, docs, panel), bf16),
            pltpu.VMEM((panel, 2 * CHAINS * docs), bf16),
            pltpu.VMEM((2, panel, topics), bf16),
            pltpu.VMEM((ny, 2, CHAINS, sub, topics), bf16),
            pltpu.VMEM((CHAINS, sub, topics), f32),
            pltpu.VMEM((CHAINS, docs, topics), f32),
            pltpu.VMEM((CHAINS, ny, sub // 2, topics), i32),
            pltpu.VMEM((CHAINS, ny, 1, topics), i32),
            pltpu.VMEM((CHAINS, ny, sub // 2, topics), i32),
            pltpu.VMEM((CHAINS, ny, 1, topics), i32),
            pltpu.VMEM((nz * share, topics), f32),
            pltpu.VMEM((nx, nz, share // 2, topics), i32),
            pltpu.VMEM((nx, nz, 1, topics), i32),
            pltpu.VMEM((nx, nz, share // 2, topics), i32),
            pltpu.VMEM((nx, nz, 1, topics), i32),
            pltpu.VMEM((nz, share // 2, topics), i32),
            pltpu.VMEM((nz, 1, topics), i32),
            pltpu.VMEM((nz, share // 2, topics), i32),
            pltpu.VMEM((nz, 1, topics), i32),
            pltpu.VMEM((ny, 1, topics), f32),
            pltpu.VMEM((2, 1, topics), f32),
            pltpu.VMEM((nx, 1, topics), f32),
            pltpu.VMEM((nz, 1, topics), f32),
            dma((5,)), dma((ny,)), dma((2,)),
            dma((nz,)), dma((nz,)), dma((nx, nz)), dma((nx, nz)), dma((nx,)), dma((nx,)),
            dma((CHAINS, ny)), dma((CHAINS, ny)), dma((CHAINS, ny)), dma((CHAINS, ny)),
            dma((CHAINS, ny)), dma((CHAINS, ny)),
            dma((CHAINS,)), dma((CHAINS,)),
            dma((nx, nz)), dma((nx, nz)), dma((nx,)), dma((nx,)),
            dma((nz,)), dma((nz,)), dma((nz,)), dma((nz,)),
            dma((ny,)), dma((ny,)), dma, dma, dma((nx,)), dma((nx,)), dma((nz,)), dma((nz,)),
        ],
        compiler_params=pltpu.CompilerParams(
            collective_id=0, has_side_effects=True, vmem_limit_bytes=VMEM_LIMIT
        ),
    )(tile_doc, tile_word, tile_live, counts, doc_init, topic_word, topic_mass[None, :], noise)


def solution(mesh):
    return jax.shard_map(
        shards,
        mesh=mesh,
        in_specs=(
            P("dp", "vocab", None, None, None),
            P("dp", "vocab", None),
            P("dp", "vocab", None),
            P("dp", "vocab"),
            P("dp", None),
            P(("vocab", "dp"), None),
            P(),
            P(("vocab", "dp"), None),
        ),
        out_specs=(P(("dp", "vocab"), None), P(("vocab", "dp"), None)),
        check_vma=False,
    )
```

```python
import functools

import jax
import jax.numpy as jnp
from jax import lax
from jax.experimental import pallas as pl
from jax.experimental.pallas import tpu as pltpu
from jax.sharding import PartitionSpec as P

ITERS = 3
ALPHA_PRIOR = 0.1
BETA_PRIOR = 0.01
HALF_STEP = 0.05
GRAD_SCALE = 16.0
MESH = pl.DeviceIdType.MESH
CHAINS = 2
CODES = 65535.0
SCALE_STEPS = 1024.0
X_CHIPS = 4
VMEM_LIMIT = 58 * 2**20


def far_first(count):
    return sorted(range(1, count), key=lambda j: -min(j, count - j))


def near_first(count):
    return sorted(range(1, count), key=lambda j: min(j, count - j))


def nt_dot(a, b):
    return lax.dot_general(a, b, (((1,), (1,)), ((), ())), preferred_element_type=jnp.float32)


def pack(values):
    half = values.shape[0] // 2
    top = jnp.maximum(jnp.max(values, axis=0, keepdims=True), 1e-30)
    scale = (jnp.log2(top) * SCALE_STEPS + 1.0).astype(jnp.int32)
    factor = jnp.exp2(scale.astype(jnp.float32) * (-1.0 / SCALE_STEPS)) * CODES
    code = jnp.minimum(values * factor + 0.5, CODES).astype(jnp.int32)
    return code[:half] | (code[half:] << 16), scale


def store_packed(ref, scale_ref, values):
    ref[...], scale_ref[...] = pack(values)


def unpack(ref, scale_ref):
    code = ref[...]
    unit = jnp.exp2(scale_ref[...].astype(jnp.float32) * (1.0 / SCALE_STEPS)) * (1.0 / CODES)
    both = jnp.concatenate([code & 0xFFFF, (code >> 16) & 0xFFFF], axis=0)
    return both.astype(jnp.float32) * unit


def body(
    nx, nz, ny, share,
    doc_table, word_table, live_table, counts_hbm, doc_hbm, word_hbm, mass_hbm, noise_hbm,
    doc_out, word_out,
    doc_pick, word_pick, live, slot_vm, slot_ref, cbuf, dbuf, word_ref, mass_ref, noise_ref,
    cnt, cnt_sib, cnt_t, prob, gall, gam, part, part_go, part_sc, got, got_sc,
    hits, hits_go, hits_sc, got_x, got_xs, sum_go, sum_sc, got_z, got_zs,
    tot_y, tot_c, tot_x, tot_z,
    in_sem, doc_sem, cnt_sem,
    pz_s, pz_r, px_s, px_r, pc_s, pc_r,
    s_s, s_r, sc_s, sc_r, g_s, g_r, gc_s, gc_r,
    hx_s, hx_r, xs_s, xs_r, hz_s, hz_r, zs_s, zs_r,
    ty_s, ty_r, tc_s, tc_r, tx_s, tx_r, tz_s, tz_r,
):
    slots, block = counts_hbm.shape[2], counts_hbm.shape[3]
    panel, topics = prob.shape[1], prob.shape[2]
    wblocks = panel // block
    rows_x = nz * share
    sub = share // CHAINS
    docs = ny * sub
    dp = lax.axis_index("dp")
    vo = lax.axis_index("vocab")
    x, z = dp // nz, lax.rem(dp, nz)
    y, c = vo // 2, lax.rem(vo, 2)
    sib = 1 - c

    def at_y(j):
        return (dp, lax.rem(y + j, ny) * 2 + c)

    def at_x(j):
        return (lax.rem(x + j, nx) * nz + z, vo)

    def at_z(j):
        return (x * nz + lax.rem(z + j, nz), vo)

    at_c = (dp, y * 2 + sib)

    def remote(src, dst, s, r, to):
        return pltpu.make_async_remote_copy(
            src_ref=src, dst_ref=dst, send_sem=s, recv_sem=r, device_id=to, device_id_type=MESH
        )

    word_in = pltpu.make_async_copy(word_hbm, word_ref, in_sem.at[0])
    mass_in = pltpu.make_async_copy(mass_hbm, mass_ref, in_sem.at[1])
    word_in.start()
    mass_in.start()

    barrier = pltpu.get_barrier_semaphore()
    peers = [at_y(j) for j in range(1, ny)] + [at_c]
    peers += [at_x(j) for j in range(1, nx)] + [at_z(j) for j in range(1, nz)]
    for to in peers:
        pl.semaphore_signal(barrier, inc=1, device_id=to, device_id_type=MESH)

    tables = [
        pltpu.make_async_copy(src, dst, in_sem.at[5 + i])
        for i, (src, dst) in enumerate(
            ((doc_table, doc_pick), (word_table, word_pick), (live_table, live))
        )
    ]
    for copy in tables:
        copy.start()
    counts_in = pltpu.make_async_copy(counts_hbm.at[0, 0], cbuf.at[pl.ds(0, slots)], in_sem.at[2])
    counts_in.start()
    doc_in = [
        pltpu.make_async_copy(
            doc_hbm.at[pl.ds((2 * q + c) * share, share)], dbuf.at[q], doc_sem.at[q]
        )
        for q in range(ny)
    ]
    for copy in doc_in:
        copy.start()
    noise_in = pltpu.make_async_copy(noise_hbm, noise_ref, in_sem.at[3])
    noise_in.start()

    def word_rows(jx, jz):
        row = (lax.rem(x - jx + nx, nx) * nz + lax.rem(z - jz + nz, nz)) * share
        return pl.ds(pl.multiple_of(row, share), share)

    def word_block(jx):
        return pl.ds(pl.multiple_of(lax.rem(x - jx + nx, nx) * rows_x, rows_x), rows_x)

    def shard(jx, jz):
        return prob.at[c, word_rows(jx, jz)]

    word_in.wait()
    mass_in.wait()
    prob[c, word_rows(0, 0), :] = (word_ref[...] / mass_ref[...]).astype(jnp.bfloat16)
    pl.semaphore_wait(barrier, len(peers))

    pz = {j: remote(shard(0, 0), shard(0, 0), pz_s.at[j], pz_r.at[j], at_z(j)) for j in range(1, nz)}
    px = {
        (jx, jz): remote(shard(0, jz), shard(0, jz), px_s.at[jx, jz], px_r.at[jx, jz], at_x(jx))
        for jx in range(1, nx)
        for jz in range(nz)
    }
    pc = [
        remote(prob.at[c, word_block(jx)], prob.at[c, word_block(jx)], pc_s.at[jx], pc_r.at[jx], at_c)
        for jx in range(nx)
    ]
    for j in near_first(nz):
        pz[j].start()
    for jx in far_first(nx):
        px[jx, 0].start()

    for copy in tables:
        copy.wait()
    lane = lax.broadcasted_iota(jnp.int32, (1, 128), 1)
    slot_of = jnp.full((1, 128), slots, jnp.int32)
    for s in range(slots):
        key = doc_pick[0, 0, s] * wblocks + word_pick[0, 0, s]
        use = jnp.where(s < live[0, 0], s, slots)
        slot_of = jnp.where(lane == key, use, slot_of)
    slot_vm[...] = slot_of
    slot_in = pltpu.make_async_copy(slot_vm, slot_ref, in_sem.at[4])
    slot_in.start()

    for copy in doc_in:
        copy.wait()
    for h in range(CHAINS):
        for q in range(ny):
            gall[q, c, h] = dbuf[q, h * sub:(h + 1) * sub, :].astype(jnp.bfloat16)
        gam[h] = dbuf[y, h * sub:(h + 1) * sub, :]

    for jz in near_first(nz):
        remote(shard(0, jz), shard(0, jz), pz_s.at[jz], pz_r.at[jz], at_z(jz)).wait_recv()
        for jx in far_first(nx):
            px[jx, jz].start()
    pc[0].start()

    counts_in.wait()
    slot_in.wait()
    cbuf[slots] = jnp.zeros((block, block), jnp.int32)
    pairs = block // share // 2

    def place(t, _):
        d, w = t // wblocks, lax.rem(t, wblocks)
        slot = slot_ref[0, t]
        col = pl.ds(pl.multiple_of(w * block, block), block)
        for k in range(pairs):
            for other in range(2):
                core = sib if other else c
                piece = cbuf[slot, pl.ds(pl.multiple_of((2 * k + core) * share, share), share), :]
                piece = piece.astype(jnp.float32).astype(jnp.bfloat16)
                for h in range(CHAINS):
                    row = pl.ds(pl.multiple_of((d * pairs + k) * sub, sub), sub)
                    val = piece[h * sub:(h + 1) * sub]
                    if other:
                        cnt_sib[h, row, col] = val
                    else:
                        cnt[c, h, row, col] = val
        return 0

    lax.fori_loop(0, slots, place, 0)
    cnt_go = remote(cnt_sib, cnt.at[c], cnt_sem.at[0], cnt_sem.at[1], at_c)
    cnt_go.start()

    def turn(w, _):
        row = pl.ds(pl.multiple_of(w * block, block), block)
        for d in range(slots // wblocks):
            tile = cbuf[slot_ref[0, d * wblocks + w]].astype(jnp.float32)
            cnt_t[row, d * block:(d + 1) * block] = tile.T.astype(jnp.bfloat16)
        return 0

    lax.fori_loop(0, wblocks, turn, 0)

    def chain_gamma(h):
        return jnp.concatenate([gall[q, c, h] for q in range(ny)], axis=0)

    both = jnp.concatenate([chain_gamma(h) for h in range(CHAINS)], axis=0)

    def first_sums(side, jx, first):
        words = word_block(jx)
        p = prob[side, words, :]
        n = jnp.concatenate([cnt[side, h, :, words] for h in range(CHAINS)], axis=0)
        ratios = (n.astype(jnp.float32) / nt_dot(both, p)).astype(jnp.bfloat16)
        add = jnp.dot(ratios, p, preferred_element_type=jnp.float32)
        for h in range(CHAINS):
            if first:
                part[h] = add[h * docs:(h + 1) * docs]
            else:
                part[h] += add[h * docs:(h + 1) * docs]

    def sib_sums(jx):
        theirs = prob.at[sib, word_block(jx)]
        remote(theirs, theirs, pc_s.at[jx], pc_r.at[jx], at_c).wait_recv()
        first_sums(sib, jx, False)

    first_sums(c, 0, True)
    remote(cnt_sib, cnt.at[sib], cnt_sem.at[0], cnt_sem.at[1], at_c).wait_recv()
    sib_sums(0)
    before = None
    for jx in near_first(nx):
        for jz in [0] + near_first(nz):
            remote(shard(jx, jz), shard(jx, jz), px_s.at[jx, jz], px_r.at[jx, jz], at_x(jx)).wait_recv()
        pc[jx].start()
        first_sums(c, jx, False)
        if before is not None:
            sib_sums(before)
        before = jx
    sib_sums(before)

    chunk = min(512, panel)

    def partial_sums(h):
        g = chain_gamma(h)
        total = None
        for side in range(2):
            for k in range(panel // chunk):
                words = pl.ds(k * chunk, chunk)
                p = prob[side, words, :]
                n = cnt[side, h, :, words].astype(jnp.float32)
                ratios = (n / nt_dot(g, p)).astype(jnp.bfloat16)
                add = jnp.dot(ratios, p, preferred_element_type=jnp.float32)
                total = add if total is None else total + add
        part[h] = total

    def doc_rows(j):
        return pl.ds(pl.multiple_of(lax.rem(y + j + ny, ny) * sub, sub), sub)

    def send_sums(h, j):
        to = lax.rem(y + j, ny)
        return remote(part_go.at[h, to], got.at[h, j], s_s.at[h, j], s_r.at[h, j], at_y(j))

    def send_scale(h, j):
        to = lax.rem(y + j, ny)
        return remote(part_sc.at[h, to], got_sc.at[h, j], sc_s.at[h, j], sc_r.at[h, j], at_y(j))

    def pack_sums(h):
        for q in range(ny):
            rows = slice(q * sub, (q + 1) * sub)
            here = part[h, rows, :] * gall[q, c, h].astype(jnp.float32)
            store_packed(part_go.at[h, q], part_sc.at[h, q], here)

    def send_gamma(h, j):
        own = gall.at[y, c, h]
        return remote(own, own, g_s.at[h, j], g_r.at[h, j], at_y(j))

    def wait_gamma(h, j):
        theirs = gall.at[lax.rem(y - j + ny, ny), c, h]
        remote(theirs, theirs, g_s.at[h, j], g_r.at[h, j], at_y(j)).wait_recv()

    for it in range(ITERS):
        for h in range(CHAINS):
            if it:
                for j in near_first(ny):
                    wait_gamma(h, j)
                for j in range(1, ny):
                    send_sums(h, j).wait_send()
                    send_scale(h, j).wait_send()
                partial_sums(h)
            pack_sums(h)
            for j in far_first(ny):
                send_scale(h, j).start()
                send_sums(h, j).start()
        for h in range(CHAINS):
            total = None
            for j in near_first(ny):
                send_scale(h, j).wait_recv()
                send_sums(h, j).wait_recv()
                add = unpack(got.at[h, j], got_sc.at[h, j])
                total = add if total is None else total + add
            total = part[h, doc_rows(0), :] + total / gall[y, c, h].astype(jnp.float32)
            gam[h] = ALPHA_PRIOR + gam[h] * total
            if it:
                for j in range(1, ny):
                    send_gamma(h, j).wait_send()
            gall[y, c, h] = gam[h].astype(jnp.bfloat16)
            for j in far_first(ny):
                send_gamma(h, j).start()

    final = jnp.concatenate([gam[h] for h in range(CHAINS)], axis=0)
    tot_y[0] = jnp.sum(final - ALPHA_PRIOR, axis=0, keepdims=True)

    def send_ty(j):
        return remote(tot_y.at[0], tot_y.at[j], ty_s.at[j], ty_r.at[j], at_y(j))

    for j in far_first(ny):
        send_ty(j).start()
    doc_out[...] = final / (jnp.sum(final, axis=1, keepdims=True) / topics)

    def give(h):
        mine = gall.at[:, c, h]
        return remote(mine, mine, gc_s.at[h], gc_r.at[h], at_c)

    def wait_give(h):
        theirs = gall.at[:, sib, h]
        remote(theirs, theirs, gc_s.at[h], gc_r.at[h], at_c).wait_recv()

    for h in range(CHAINS):
        for j in near_first(ny):
            wait_gamma(h, j)
        give(h).start()
    total = tot_y[0]
    for j in near_first(ny):
        send_ty(j).wait_recv()
        total = total + tot_y[j]
    tot_c[0] = total
    send_tc = remote(tot_c.at[0], tot_c.at[1], tc_s, tc_r, at_c)
    send_tc.start()
    for h in range(CHAINS):
        wait_give(h)

    def z_rows(j):
        return pl.ds(pl.multiple_of(lax.rem(z + j, nz) * share, share), share)

    def send_hx(jx, jz):
        return remote(
            hits_go.at[jx, lax.rem(z + jz, nz)], got_x.at[jx, jz],
            hx_s.at[jx, jz], hx_r.at[jx, jz], at_x(jx),
        )

    def send_xs(jx):
        return remote(hits_sc.at[jx], got_xs.at[jx], xs_s.at[jx], xs_r.at[jx], at_x(jx))

    def send_zs(j):
        return remote(sum_sc.at[j], got_zs.at[j], zs_s.at[j], zs_r.at[j], at_z(j))

    def send_hz(j):
        return remote(sum_go.at[j], got_z.at[j], hz_s.at[j], hz_r.at[j], at_z(j))

    def send_tx(j):
        return remote(tot_x.at[0], tot_x.at[j], tx_s.at[j], tx_r.at[j], at_x(j))

    def send_tz(j):
        return remote(tot_z.at[0], tot_z.at[j], tz_s.at[j], tz_r.at[j], at_z(j))

    send_tc.wait_recv()
    tot_x[0] = tot_c[0] + tot_c[1]
    for j in far_first(nx):
        send_tx(j).start()
    gamma_all = gall[...].reshape(2 * CHAINS * docs, topics)
    z_order, x_order = far_first(nz) + [0], far_first(nx)
    early = nz // 2
    for jx in x_order + [0]:
        words = word_block(nx - jx)
        p = prob[c, words, :]
        ratios = (cnt_t[words, :].astype(jnp.float32) / nt_dot(p, gamma_all)).astype(jnp.bfloat16)
        found = jnp.dot(ratios, gamma_all, preferred_element_type=jnp.float32) * p.astype(jnp.float32)
        if not jx:
            hits[...] = found
        else:
            for q in range(nz):
                store_packed(hits_go.at[jx, q], hits_sc.at[jx, q], found[q * share:(q + 1) * share])
            send_xs(jx).start()
            if jx == x_order[0]:
                for jz in z_order[:early]:
                    send_hx(jx, jz).start()
            if jx == x_order[-1]:
                for jz in z_order:
                    for to in x_order:
                        if to != x_order[0] or jz not in z_order[:early]:
                            send_hx(to, jz).start()

    total = tot_x[0]
    for j in near_first(nx):
        send_tx(j).wait_recv()
        total = total + tot_x[j]
    tot_z[0] = total
    for j in far_first(nz):
        send_tz(j).start()

    for jx in far_first(nx):
        send_xs(jx).wait_recv()
    for jz in z_order:
        total = hits[z_rows(jz), :]
        for jx in range(1, nx):
            send_hx(jx, jz).wait_recv()
            total = total + unpack(got_x.at[jx, jz], got_xs.at[jx, lax.rem(z + jz, nz)])
        if jz:
            store_packed(sum_go.at[jz], sum_sc.at[jz], total)
            send_zs(jz).start()
            send_hz(jz).start()
    reduced = total

    totals = tot_z[0]
    for j in near_first(nz):
        send_tz(j).wait_recv()
        totals = totals + tot_z[j]
    noise_in.wait()
    for j in near_first(nz):
        send_zs(j).wait_recv()
        send_hz(j).wait_recv()
        reduced = reduced + unpack(got_z.at[j], got_zs.at[j])
    word = word_ref[...]
    probs = word / mass_ref[...]
    counted = reduced * (probs / prob[c, word_rows(0, 0), :].astype(jnp.float32))
    drift = BETA_PRIOR - word + GRAD_SCALE * (counted - totals * probs)
    word_out[...] = jnp.abs(word + HALF_STEP * drift + jnp.sqrt(word) * noise_ref[...])

    for j in range(1, nz):
        pz[j].wait_send()
        send_hz(j).wait_send()
        send_zs(j).wait_send()
        send_tz(j).wait_send()
    for jx in range(1, nx):
        send_tx(jx).wait_send()
        send_xs(jx).wait_send()
        for jz in range(nz):
            px[jx, jz].wait_send()
            send_hx(jx, jz).wait_send()
    for jx in range(nx):
        pc[jx].wait_send()
    cnt_go.wait_send()
    send_tc.wait_send()
    for h in range(CHAINS):
        give(h).wait_send()
        for j in range(1, ny):
            send_sums(h, j).wait_send()
            send_scale(h, j).wait_send()
            send_gamma(h, j).wait_send()
    for j in range(1, ny):
        send_ty(j).wait_send()


def shards(counts, tile_doc, tile_word, tile_live, doc_init, topic_word, topic_mass, noise):
    topics = topic_mass.shape[0]
    slots, block = counts.shape[2], counts.shape[3]
    n_dp, n_vocab = lax.axis_size("dp"), lax.axis_size("vocab")
    nx = X_CHIPS
    nz, ny = n_dp // nx, n_vocab // 2
    share = topic_word.shape[0]
    panel = share * n_dp
    sub = share // CHAINS
    docs = ny * sub

    f32, bf16, i32, dma = jnp.float32, jnp.bfloat16, jnp.int32, pltpu.SemaphoreType.DMA
    vmem = pl.BlockSpec(memory_space=pltpu.VMEM)
    hbm = pl.BlockSpec(memory_space=pl.ANY)
    return pl.pallas_call(
        functools.partial(body, nx, nz, ny, share),
        out_shape=(
            jax.ShapeDtypeStruct((share, topics), f32),
            jax.ShapeDtypeStruct((share, topics), f32),
        ),
        in_specs=[hbm, hbm, hbm, hbm, hbm, hbm, hbm, hbm],
        out_specs=(vmem, vmem),
        scratch_shapes=[
            pltpu.SMEM((1, 1, slots), i32),
            pltpu.SMEM((1, 1, slots), i32),
            pltpu.SMEM((1, 1), i32),
            pltpu.VMEM((1, 128), jnp.int32),
            pltpu.SMEM((1, 128), jnp.int32),
            pltpu.VMEM((slots + 1, block, block), jnp.int32),
            pltpu.VMEM((ny, share, topics), f32),
            pltpu.VMEM((share, topics), f32),
            pltpu.VMEM((1, topics), f32),
            pltpu.VMEM((share, topics), f32),
            pltpu.VMEM((2, CHAINS, docs, panel), bf16),
            pltpu.VMEM((CHAINS, docs, panel), bf16),
            pltpu.VMEM((panel, 2 * CHAINS * docs), bf16),
            pltpu.VMEM((2, panel, topics), bf16),
            pltpu.VMEM((ny, 2, CHAINS, sub, topics), bf16),
            pltpu.VMEM((CHAINS, sub, topics), f32),
            pltpu.VMEM((CHAINS, docs, topics), f32),
            pltpu.VMEM((CHAINS, ny, sub // 2, topics), i32),
            pltpu.VMEM((CHAINS, ny, 1, topics), i32),
            pltpu.VMEM((CHAINS, ny, sub // 2, topics), i32),
            pltpu.VMEM((CHAINS, ny, 1, topics), i32),
            pltpu.VMEM((nz * share, topics), f32),
            pltpu.VMEM((nx, nz, share // 2, topics), i32),
            pltpu.VMEM((nx, nz, 1, topics), i32),
            pltpu.VMEM((nx, nz, share // 2, topics), i32),
            pltpu.VMEM((nx, nz, 1, topics), i32),
            pltpu.VMEM((nz, share // 2, topics), i32),
            pltpu.VMEM((nz, 1, topics), i32),
            pltpu.VMEM((nz, share // 2, topics), i32),
            pltpu.VMEM((nz, 1, topics), i32),
            pltpu.VMEM((ny, 1, topics), f32),
            pltpu.VMEM((2, 1, topics), f32),
            pltpu.VMEM((nx, 1, topics), f32),
            pltpu.VMEM((nz, 1, topics), f32),
            dma((8,)), dma((ny,)), dma((2,)),
            dma((nz,)), dma((nz,)), dma((nx, nz)), dma((nx, nz)), dma((nx,)), dma((nx,)),
            dma((CHAINS, ny)), dma((CHAINS, ny)), dma((CHAINS, ny)), dma((CHAINS, ny)),
            dma((CHAINS, ny)), dma((CHAINS, ny)),
            dma((CHAINS,)), dma((CHAINS,)),
            dma((nx, nz)), dma((nx, nz)), dma((nx,)), dma((nx,)),
            dma((nz,)), dma((nz,)), dma((nz,)), dma((nz,)),
            dma((ny,)), dma((ny,)), dma, dma, dma((nx,)), dma((nx,)), dma((nz,)), dma((nz,)),
        ],
        compiler_params=pltpu.CompilerParams(
            collective_id=0, has_side_effects=True, vmem_limit_bytes=VMEM_LIMIT
        ),
    )(tile_doc, tile_word, tile_live, counts, doc_init, topic_word, topic_mass[None, :], noise)


def solution(mesh):
    return jax.shard_map(
        shards,
        mesh=mesh,
        in_specs=(
            P("dp", "vocab", None, None, None),
            P("dp", "vocab", None),
            P("dp", "vocab", None),
            P("dp", "vocab"),
            P("dp", None),
            P(("vocab", "dp"), None),
            P(),
            P(("vocab", "dp"), None),
        ),
        out_specs=(P(("dp", "vocab"), None), P(("vocab", "dp"), None)),
        check_vma=False,
    )
```

```python
import functools

import jax
import jax.numpy as jnp
from jax import lax
from jax.experimental import pallas as pl
from jax.experimental.pallas import tpu as pltpu
from jax.sharding import PartitionSpec as P

ITERS = 3
ALPHA_PRIOR = 0.1
BETA_PRIOR = 0.01
HALF_STEP = 0.05
GRAD_SCALE = 16.0
MESH = pl.DeviceIdType.MESH
CHAINS = 2
CODES = 65535.0
SCALE_STEPS = 1024.0
X_CHIPS = 4
VMEM_LIMIT = 58 * 2**20


def far_first(count):
    return sorted(range(1, count), key=lambda j: -min(j, count - j))


def near_first(count):
    return sorted(range(1, count), key=lambda j: min(j, count - j))


def nt_dot(a, b):
    return lax.dot_general(a, b, (((1,), (1,)), ((), ())), preferred_element_type=jnp.float32)


def pack(values):
    half = values.shape[0] // 2
    top = jnp.maximum(jnp.max(values, axis=0, keepdims=True), 1e-30)
    scale = (jnp.log2(top) * SCALE_STEPS + 1.0).astype(jnp.int32)
    factor = jnp.exp2(scale.astype(jnp.float32) * (-1.0 / SCALE_STEPS)) * CODES
    code = jnp.minimum(values * factor + 0.5, CODES).astype(jnp.int32)
    return code[:half] | (code[half:] << 16), scale


def store_packed(ref, scale_ref, values):
    ref[...], scale_ref[...] = pack(values)


def unpack(ref, scale_ref):
    code = ref[...]
    unit = jnp.exp2(scale_ref[...].astype(jnp.float32) * (1.0 / SCALE_STEPS)) * (1.0 / CODES)
    both = jnp.concatenate([code & 0xFFFF, (code >> 16) & 0xFFFF], axis=0)
    return both.astype(jnp.float32) * unit


def body(
    nx, nz, ny, share,
    doc_table, word_table, live_table, counts_hbm, doc_hbm, word_hbm, mass_hbm, noise_hbm,
    doc_out, word_out,
    doc_pick, word_pick, live, slot_vm, slot_ref, cbuf, dbuf, word_ref, mass_ref, noise_ref,
    cnt, cnt_sib, cnt_t, prob, gall, gam, part, part_go, part_sc, got, got_sc,
    hits, hits_go, hits_sc, got_x, got_xs, sum_go, sum_sc, got_z, got_zs,
    tot_y, tot_c, tot_x, tot_z,
    in_sem, doc_sem, cnt_sem,
    pz_s, pz_r, px_s, px_r, pc_s, pc_r,
    s_s, s_r, sc_s, sc_r, g_s, g_r, gc_s, gc_r,
    hx_s, hx_r, xs_s, xs_r, hz_s, hz_r, zs_s, zs_r,
    ty_s, ty_r, tc_s, tc_r, tx_s, tx_r, tz_s, tz_r,
):
    slots, block = counts_hbm.shape[2], counts_hbm.shape[3]
    panel, topics = prob.shape[1], prob.shape[2]
    wblocks = panel // block
    rows_x = nz * share
    sub = share // CHAINS
    docs = ny * sub
    dp = lax.axis_index("dp")
    vo = lax.axis_index("vocab")
    x, z = dp // nz, lax.rem(dp, nz)
    y, c = vo // 2, lax.rem(vo, 2)
    sib = 1 - c

    def at_y(j):
        return (dp, lax.rem(y + j, ny) * 2 + c)

    def at_x(j):
        return (lax.rem(x + j, nx) * nz + z, vo)

    def at_z(j):
        return (x * nz + lax.rem(z + j, nz), vo)

    at_c = (dp, y * 2 + sib)

    def remote(src, dst, s, r, to):
        return pltpu.make_async_remote_copy(
            src_ref=src, dst_ref=dst, send_sem=s, recv_sem=r, device_id=to, device_id_type=MESH
        )

    word_in = pltpu.make_async_copy(word_hbm, word_ref, in_sem.at[0])
    mass_in = pltpu.make_async_copy(mass_hbm, mass_ref, in_sem.at[1])
    word_in.start()
    mass_in.start()

    barrier = pltpu.get_barrier_semaphore()
    peers = [at_y(j) for j in range(1, ny)] + [at_c]
    peers += [at_x(j) for j in range(1, nx)] + [at_z(j) for j in range(1, nz)]
    for to in peers:
        pl.semaphore_signal(barrier, inc=1, device_id=to, device_id_type=MESH)

    tables = [
        pltpu.make_async_copy(src, dst, in_sem.at[5 + i])
        for i, (src, dst) in enumerate(
            ((doc_table, doc_pick), (word_table, word_pick), (live_table, live))
        )
    ]
    for copy in tables:
        copy.start()
    counts_in = pltpu.make_async_copy(counts_hbm.at[0, 0], cbuf.at[pl.ds(0, slots)], in_sem.at[2])
    counts_in.start()
    doc_in = [
        pltpu.make_async_copy(
            doc_hbm.at[pl.ds((2 * q + c) * share, share)], dbuf.at[q], doc_sem.at[q]
        )
        for q in range(ny)
    ]
    for copy in doc_in:
        copy.start()
    noise_in = pltpu.make_async_copy(noise_hbm, noise_ref, in_sem.at[3])
    noise_in.start()

    def word_rows(jx, jz):
        row = (lax.rem(x - jx + nx, nx) * nz + lax.rem(z - jz + nz, nz)) * share
        return pl.ds(pl.multiple_of(row, share), share)

    def word_block(jx):
        return pl.ds(pl.multiple_of(lax.rem(x - jx + nx, nx) * rows_x, rows_x), rows_x)

    def shard(jx, jz):
        return prob.at[c, word_rows(jx, jz)]

    word_in.wait()
    mass_in.wait()
    prob[c, word_rows(0, 0), :] = (word_ref[...] / mass_ref[...]).astype(jnp.bfloat16)
    pl.semaphore_wait(barrier, len(peers))

    pz = {j: remote(shard(0, 0), shard(0, 0), pz_s.at[j], pz_r.at[j], at_z(j)) for j in range(1, nz)}
    px = {
        (jx, jz): remote(shard(0, jz), shard(0, jz), px_s.at[jx, jz], px_r.at[jx, jz], at_x(jx))
        for jx in range(1, nx)
        for jz in range(nz)
    }
    pc = [
        remote(prob.at[c, word_block(jx)], prob.at[c, word_block(jx)], pc_s.at[jx], pc_r.at[jx], at_c)
        for jx in range(nx)
    ]
    for j in near_first(nz):
        pz[j].start()
    for jx in far_first(nx):
        px[jx, 0].start()

    for copy in tables:
        copy.wait()
    lane = lax.broadcasted_iota(jnp.int32, (1, 128), 1)
    slot_of = jnp.full((1, 128), slots, jnp.int32)
    for s in range(slots):
        key = doc_pick[0, 0, s] * wblocks + word_pick[0, 0, s]
        use = jnp.where(s < live[0, 0], s, slots)
        slot_of = jnp.where(lane == key, use, slot_of)
    slot_vm[...] = slot_of
    slot_in = pltpu.make_async_copy(slot_vm, slot_ref, in_sem.at[4])
    slot_in.start()

    for copy in doc_in:
        copy.wait()
    for h in range(CHAINS):
        for q in range(ny):
            gall[q, c, h] = dbuf[q, h * sub:(h + 1) * sub, :].astype(jnp.bfloat16)
        gam[h] = dbuf[y, h * sub:(h + 1) * sub, :]

    for jz in near_first(nz):
        remote(shard(0, jz), shard(0, jz), pz_s.at[jz], pz_r.at[jz], at_z(jz)).wait_recv()
        for jx in far_first(nx):
            px[jx, jz].start()
    pc[0].start()

    counts_in.wait()
    slot_in.wait()
    cbuf[slots] = jnp.zeros((block, block), jnp.int32)
    pairs = block // share // 2

    def place(t, _):
        d, w = t // wblocks, lax.rem(t, wblocks)
        slot = slot_ref[0, t]
        col = pl.ds(pl.multiple_of(w * block, block), block)
        for k in range(pairs):
            for other in range(2):
                core = sib if other else c
                piece = cbuf[slot, pl.ds(pl.multiple_of((2 * k + core) * share, share), share), :]
                piece = piece.astype(jnp.float32).astype(jnp.bfloat16)
                for h in range(CHAINS):
                    row = pl.ds(pl.multiple_of((d * pairs + k) * sub, sub), sub)
                    val = piece[h * sub:(h + 1) * sub]
                    if other:
                        cnt_sib[h, row, col] = val
                    else:
                        cnt[c, h, row, col] = val
        return 0

    lax.fori_loop(0, slots, place, 0)
    cnt_go = remote(cnt_sib, cnt.at[c], cnt_sem.at[0], cnt_sem.at[1], at_c)
    cnt_go.start()

    def turn(w, _):
        row = pl.ds(pl.multiple_of(w * block, block), block)
        for d in range(slots // wblocks):
            tile = cbuf[slot_ref[0, d * wblocks + w]].astype(jnp.float32)
            cnt_t[row, d * block:(d + 1) * block] = tile.T.astype(jnp.bfloat16)
        return 0

    lax.fori_loop(0, wblocks, turn, 0)

    def chain_gamma(h):
        return jnp.concatenate([gall[q, c, h] for q in range(ny)], axis=0)

    both = jnp.concatenate([chain_gamma(h) for h in range(CHAINS)], axis=0)

    def first_sums(side, jx, first):
        words = word_block(jx)
        p = prob[side, words, :]
        n = jnp.concatenate([cnt[side, h, :, words] for h in range(CHAINS)], axis=0)
        ratios = (n.astype(jnp.float32) / nt_dot(both, p)).astype(jnp.bfloat16)
        add = jnp.dot(ratios, p, preferred_element_type=jnp.float32)
        for h in range(CHAINS):
            if first:
                part[h] = add[h * docs:(h + 1) * docs]
            else:
                part[h] += add[h * docs:(h + 1) * docs]

    def sib_sums(jx):
        theirs = prob.at[sib, word_block(jx)]
        remote(theirs, theirs, pc_s.at[jx], pc_r.at[jx], at_c).wait_recv()
        first_sums(sib, jx, False)

    first_sums(c, 0, True)
    remote(cnt_sib, cnt.at[sib], cnt_sem.at[0], cnt_sem.at[1], at_c).wait_recv()
    sib_sums(0)
    before = None
    for jx in near_first(nx):
        for jz in [0] + near_first(nz):
            remote(shard(jx, jz), shard(jx, jz), px_s.at[jx, jz], px_r.at[jx, jz], at_x(jx)).wait_recv()
        pc[jx].start()
        first_sums(c, jx, False)
        if before is not None:
            sib_sums(before)
        before = jx
    sib_sums(before)

    chunk = min(512, panel)

    def partial_sums(h):
        g = chain_gamma(h)
        total = None
        for side in range(2):
            for k in range(panel // chunk):
                words = pl.ds(k * chunk, chunk)
                p = prob[side, words, :]
                n = cnt[side, h, :, words].astype(jnp.float32)
                ratios = (n / nt_dot(g, p)).astype(jnp.bfloat16)
                add = jnp.dot(ratios, p, preferred_element_type=jnp.float32)
                total = add if total is None else total + add
        part[h] = total

    def doc_rows(j):
        return pl.ds(pl.multiple_of(lax.rem(y + j + ny, ny) * sub, sub), sub)

    def send_sums(h, j):
        to = lax.rem(y + j, ny)
        return remote(part_go.at[h, to], got.at[h, j], s_s.at[h, j], s_r.at[h, j], at_y(j))

    def send_scale(h, j):
        to = lax.rem(y + j, ny)
        return remote(part_sc.at[h, to], got_sc.at[h, j], sc_s.at[h, j], sc_r.at[h, j], at_y(j))

    def pack_sums(h):
        for q in range(ny):
            rows = slice(q * sub, (q + 1) * sub)
            here = part[h, rows, :] * gall[q, c, h].astype(jnp.float32)
            store_packed(part_go.at[h, q], part_sc.at[h, q], here)

    def send_gamma(h, j):
        own = gall.at[y, c, h]
        return remote(own, own, g_s.at[h, j], g_r.at[h, j], at_y(j))

    def wait_gamma(h, j):
        theirs = gall.at[lax.rem(y - j + ny, ny), c, h]
        remote(theirs, theirs, g_s.at[h, j], g_r.at[h, j], at_y(j)).wait_recv()

    for it in range(ITERS):
        for h in range(CHAINS):
            if it:
                for j in near_first(ny):
                    wait_gamma(h, j)
                for j in range(1, ny):
                    send_sums(h, j).wait_send()
                    send_scale(h, j).wait_send()
                partial_sums(h)
            pack_sums(h)
            for j in far_first(ny):
                send_scale(h, j).start()
            for j in far_first(ny):
                send_sums(h, j).start()
        for h in range(CHAINS):
            total = None
            for j in near_first(ny):
                send_scale(h, j).wait_recv()
                send_sums(h, j).wait_recv()
                add = unpack(got.at[h, j], got_sc.at[h, j])
                total = add if total is None else total + add
            total = part[h, doc_rows(0), :] + total / gall[y, c, h].astype(jnp.float32)
            gam[h] = ALPHA_PRIOR + gam[h] * total
            if it:
                for j in range(1, ny):
                    send_gamma(h, j).wait_send()
            gall[y, c, h] = gam[h].astype(jnp.bfloat16)
            for j in far_first(ny):
                send_gamma(h, j).start()

    final = jnp.concatenate([gam[h] for h in range(CHAINS)], axis=0)
    tot_y[0] = jnp.sum(final - ALPHA_PRIOR, axis=0, keepdims=True)

    def send_ty(j):
        return remote(tot_y.at[0], tot_y.at[j], ty_s.at[j], ty_r.at[j], at_y(j))

    for j in far_first(ny):
        send_ty(j).start()
    doc_out[...] = final / (jnp.sum(final, axis=1, keepdims=True) / topics)

    def give(h):
        mine = gall.at[:, c, h]
        return remote(mine, mine, gc_s.at[h], gc_r.at[h], at_c)

    def wait_give(h):
        theirs = gall.at[:, sib, h]
        remote(theirs, theirs, gc_s.at[h], gc_r.at[h], at_c).wait_recv()

    for h in range(CHAINS):
        for j in near_first(ny):
            wait_gamma(h, j)
        give(h).start()
    total = tot_y[0]
    for j in near_first(ny):
        send_ty(j).wait_recv()
        total = total + tot_y[j]
    tot_c[0] = total
    send_tc = remote(tot_c.at[0], tot_c.at[1], tc_s, tc_r, at_c)
    send_tc.start()
    for h in range(CHAINS):
        wait_give(h)

    def z_rows(j):
        return pl.ds(pl.multiple_of(lax.rem(z + j, nz) * share, share), share)

    def send_hx(jx, jz):
        return remote(
            hits_go.at[jx, lax.rem(z + jz, nz)], got_x.at[jx, jz],
            hx_s.at[jx, jz], hx_r.at[jx, jz], at_x(jx),
        )

    def send_xs(jx):
        return remote(hits_sc.at[jx], got_xs.at[jx], xs_s.at[jx], xs_r.at[jx], at_x(jx))

    def send_zs(j):
        return remote(sum_sc.at[j], got_zs.at[j], zs_s.at[j], zs_r.at[j], at_z(j))

    def send_hz(j):
        return remote(sum_go.at[j], got_z.at[j], hz_s.at[j], hz_r.at[j], at_z(j))

    def send_tx(j):
        return remote(tot_x.at[0], tot_x.at[j], tx_s.at[j], tx_r.at[j], at_x(j))

    def send_tz(j):
        return remote(tot_z.at[0], tot_z.at[j], tz_s.at[j], tz_r.at[j], at_z(j))

    send_tc.wait_recv()
    tot_x[0] = tot_c[0] + tot_c[1]
    for j in far_first(nx):
        send_tx(j).start()
    gamma_all = gall[...].reshape(2 * CHAINS * docs, topics)
    z_order, x_order = far_first(nz) + [0], far_first(nx)
    early = nz // 2
    for jx in x_order + [0]:
        words = word_block(nx - jx)
        p = prob[c, words, :]
        ratios = (cnt_t[words, :].astype(jnp.float32) / nt_dot(p, gamma_all)).astype(jnp.bfloat16)
        found = jnp.dot(ratios, gamma_all, preferred_element_type=jnp.float32) * p.astype(jnp.float32)
        if not jx:
            hits[...] = found
        else:
            for q in range(nz):
                store_packed(hits_go.at[jx, q], hits_sc.at[jx, q], found[q * share:(q + 1) * share])
            send_xs(jx).start()
            if jx == x_order[0]:
                for jz in z_order[:early]:
                    send_hx(jx, jz).start()
            if jx == x_order[-1]:
                for jz in z_order:
                    for to in x_order:
                        if to != x_order[0] or jz not in z_order[:early]:
                            send_hx(to, jz).start()

    total = tot_x[0]
    for j in near_first(nx):
        send_tx(j).wait_recv()
        total = total + tot_x[j]
    tot_z[0] = total
    for j in far_first(nz):
        send_tz(j).start()

    for jx in far_first(nx):
        send_xs(jx).wait_recv()
    for jz in z_order:
        total = hits[z_rows(jz), :]
        for jx in range(1, nx):
            send_hx(jx, jz).wait_recv()
            total = total + unpack(got_x.at[jx, jz], got_xs.at[jx, lax.rem(z + jz, nz)])
        if jz:
            store_packed(sum_go.at[jz], sum_sc.at[jz], total)
            send_zs(jz).start()
            send_hz(jz).start()
    reduced = total

    totals = tot_z[0]
    for j in near_first(nz):
        send_tz(j).wait_recv()
        totals = totals + tot_z[j]
    noise_in.wait()
    for j in near_first(nz):
        send_zs(j).wait_recv()
        send_hz(j).wait_recv()
        reduced = reduced + unpack(got_z.at[j], got_zs.at[j])
    word = word_ref[...]
    probs = word / mass_ref[...]
    counted = reduced * (probs / prob[c, word_rows(0, 0), :].astype(jnp.float32))
    drift = BETA_PRIOR - word + GRAD_SCALE * (counted - totals * probs)
    word_out[...] = jnp.abs(word + HALF_STEP * drift + jnp.sqrt(word) * noise_ref[...])

    for j in range(1, nz):
        pz[j].wait_send()
        send_hz(j).wait_send()
        send_zs(j).wait_send()
        send_tz(j).wait_send()
    for jx in range(1, nx):
        send_tx(jx).wait_send()
        send_xs(jx).wait_send()
        for jz in range(nz):
            px[jx, jz].wait_send()
            send_hx(jx, jz).wait_send()
    for jx in range(nx):
        pc[jx].wait_send()
    cnt_go.wait_send()
    send_tc.wait_send()
    for h in range(CHAINS):
        give(h).wait_send()
        for j in range(1, ny):
            send_sums(h, j).wait_send()
            send_scale(h, j).wait_send()
            send_gamma(h, j).wait_send()
    for j in range(1, ny):
        send_ty(j).wait_send()


def shards(counts, tile_doc, tile_word, tile_live, doc_init, topic_word, topic_mass, noise):
    topics = topic_mass.shape[0]
    slots, block = counts.shape[2], counts.shape[3]
    n_dp, n_vocab = lax.axis_size("dp"), lax.axis_size("vocab")
    nx = X_CHIPS
    nz, ny = n_dp // nx, n_vocab // 2
    share = topic_word.shape[0]
    panel = share * n_dp
    sub = share // CHAINS
    docs = ny * sub

    f32, bf16, i32, dma = jnp.float32, jnp.bfloat16, jnp.int32, pltpu.SemaphoreType.DMA
    vmem = pl.BlockSpec(memory_space=pltpu.VMEM)
    hbm = pl.BlockSpec(memory_space=pl.ANY)
    return pl.pallas_call(
        functools.partial(body, nx, nz, ny, share),
        out_shape=(
            jax.ShapeDtypeStruct((share, topics), f32),
            jax.ShapeDtypeStruct((share, topics), f32),
        ),
        in_specs=[hbm, hbm, hbm, hbm, hbm, hbm, hbm, hbm],
        out_specs=(vmem, vmem),
        scratch_shapes=[
            pltpu.SMEM((1, 1, slots), i32),
            pltpu.SMEM((1, 1, slots), i32),
            pltpu.SMEM((1, 1), i32),
            pltpu.VMEM((1, 128), jnp.int32),
            pltpu.SMEM((1, 128), jnp.int32),
            pltpu.VMEM((slots + 1, block, block), jnp.int32),
            pltpu.VMEM((ny, share, topics), f32),
            pltpu.VMEM((share, topics), f32),
            pltpu.VMEM((1, topics), f32),
            pltpu.VMEM((share, topics), f32),
            pltpu.VMEM((2, CHAINS, docs, panel), bf16),
            pltpu.VMEM((CHAINS, docs, panel), bf16),
            pltpu.VMEM((panel, 2 * CHAINS * docs), bf16),
            pltpu.VMEM((2, panel, topics), bf16),
            pltpu.VMEM((ny, 2, CHAINS, sub, topics), bf16),
            pltpu.VMEM((CHAINS, sub, topics), f32),
            pltpu.VMEM((CHAINS, docs, topics), f32),
            pltpu.VMEM((CHAINS, ny, sub // 2, topics), i32),
            pltpu.VMEM((CHAINS, ny, 1, topics), i32),
            pltpu.VMEM((CHAINS, ny, sub // 2, topics), i32),
            pltpu.VMEM((CHAINS, ny, 1, topics), i32),
            pltpu.VMEM((nz * share, topics), f32),
            pltpu.VMEM((nx, nz, share // 2, topics), i32),
            pltpu.VMEM((nx, nz, 1, topics), i32),
            pltpu.VMEM((nx, nz, share // 2, topics), i32),
            pltpu.VMEM((nx, nz, 1, topics), i32),
            pltpu.VMEM((nz, share // 2, topics), i32),
            pltpu.VMEM((nz, 1, topics), i32),
            pltpu.VMEM((nz, share // 2, topics), i32),
            pltpu.VMEM((nz, 1, topics), i32),
            pltpu.VMEM((ny, 1, topics), f32),
            pltpu.VMEM((2, 1, topics), f32),
            pltpu.VMEM((nx, 1, topics), f32),
            pltpu.VMEM((nz, 1, topics), f32),
            dma((8,)), dma((ny,)), dma((2,)),
            dma((nz,)), dma((nz,)), dma((nx, nz)), dma((nx, nz)), dma((nx,)), dma((nx,)),
            dma((CHAINS, ny)), dma((CHAINS, ny)), dma((CHAINS, ny)), dma((CHAINS, ny)),
            dma((CHAINS, ny)), dma((CHAINS, ny)),
            dma((CHAINS,)), dma((CHAINS,)),
            dma((nx, nz)), dma((nx, nz)), dma((nx,)), dma((nx,)),
            dma((nz,)), dma((nz,)), dma((nz,)), dma((nz,)),
            dma((ny,)), dma((ny,)), dma, dma, dma((nx,)), dma((nx,)), dma((nz,)), dma((nz,)),
        ],
        compiler_params=pltpu.CompilerParams(
            collective_id=0, has_side_effects=True, vmem_limit_bytes=VMEM_LIMIT
        ),
    )(tile_doc, tile_word, tile_live, counts, doc_init, topic_word, topic_mass[None, :], noise)


def solution(mesh):
    return jax.shard_map(
        shards,
        mesh=mesh,
        in_specs=(
            P("dp", "vocab", None, None, None),
            P("dp", "vocab", None),
            P("dp", "vocab", None),
            P("dp", "vocab"),
            P("dp", None),
            P(("vocab", "dp"), None),
            P(),
            P(("vocab", "dp"), None),
        ),
        out_specs=(P(("dp", "vocab"), None), P(("vocab", "dp"), None)),
        check_vma=False,
    )
```

```python
import functools

import jax
import jax.numpy as jnp
from jax import lax
from jax.experimental import pallas as pl
from jax.experimental.pallas import tpu as pltpu
from jax.sharding import PartitionSpec as P

ITERS = 3
ALPHA_PRIOR = 0.1
BETA_PRIOR = 0.01
HALF_STEP = 0.05
GRAD_SCALE = 16.0
MESH = pl.DeviceIdType.MESH
CHAINS = 2
CODES = 65535.0
SCALE_STEPS = 1024.0
X_CHIPS = 4
VMEM_LIMIT = 58 * 2**20


def far_first(count):
    return sorted(range(1, count), key=lambda j: -min(j, count - j))


def near_first(count):
    return sorted(range(1, count), key=lambda j: min(j, count - j))


def nt_dot(a, b):
    return lax.dot_general(a, b, (((1,), (1,)), ((), ())), preferred_element_type=jnp.float32)


def pack(values):
    half = values.shape[0] // 2
    top = jnp.maximum(jnp.max(values, axis=0, keepdims=True), 1e-30)
    scale = (jnp.log2(top) * SCALE_STEPS + 1.0).astype(jnp.int32)
    factor = jnp.exp2(scale.astype(jnp.float32) * (-1.0 / SCALE_STEPS)) * CODES
    code = jnp.minimum(values * factor + 0.5, CODES).astype(jnp.int32)
    return code[:half] | (code[half:] << 16), scale


def store_packed(ref, scale_ref, values):
    ref[...], scale_ref[...] = pack(values)


def unpack(ref, scale_ref):
    code = ref[...]
    unit = jnp.exp2(scale_ref[...].astype(jnp.float32) * (1.0 / SCALE_STEPS)) * (1.0 / CODES)
    both = jnp.concatenate([code & 0xFFFF, (code >> 16) & 0xFFFF], axis=0)
    return both.astype(jnp.float32) * unit


def body(
    nx, nz, ny, share,
    doc_table, word_table, live_table, counts_hbm, doc_hbm, word_hbm, mass_hbm, noise_hbm,
    doc_out, word_out,
    doc_pick, word_pick, live, slot_vm, slot_ref, cbuf, dbuf, word_ref, mass_ref, noise_ref,
    cnt, cnt_sib, cnt_t, prob, gall, gam, part, part_go, part_sc, got, got_sc,
    hits, hits_go, hits_sc, got_x, got_xs, sum_go, sum_sc, got_z, got_zs,
    tot_y, tot_c, tot_x, tot_z,
    in_sem, doc_sem, cnt_sem,
    pz_s, pz_r, px_s, px_r, pc_s, pc_r,
    s_s, s_r, sc_s, sc_r, g_s, g_r, gc_s, gc_r,
    hx_s, hx_r, xs_s, xs_r, hz_s, hz_r, zs_s, zs_r,
    ty_s, ty_r, tc_s, tc_r, tx_s, tx_r, tz_s, tz_r,
):
    slots, block = counts_hbm.shape[2], counts_hbm.shape[3]
    panel, topics = prob.shape[1], prob.shape[2]
    wblocks = panel // block
    rows_x = nz * share
    sub = share // CHAINS
    docs = ny * sub
    dp = lax.axis_index("dp")
    vo = lax.axis_index("vocab")
    x, z = dp // nz, lax.rem(dp, nz)
    y, c = vo // 2, lax.rem(vo, 2)
    sib = 1 - c

    def at_y(j):
        return (dp, lax.rem(y + j, ny) * 2 + c)

    def at_x(j):
        return (lax.rem(x + j, nx) * nz + z, vo)

    def at_z(j):
        return (x * nz + lax.rem(z + j, nz), vo)

    at_c = (dp, y * 2 + sib)

    def remote(src, dst, s, r, to):
        return pltpu.make_async_remote_copy(
            src_ref=src, dst_ref=dst, send_sem=s, recv_sem=r, device_id=to, device_id_type=MESH
        )

    word_in = pltpu.make_async_copy(word_hbm, word_ref, in_sem.at[0])
    mass_in = pltpu.make_async_copy(mass_hbm, mass_ref, in_sem.at[1])
    word_in.start()
    mass_in.start()

    barrier = pltpu.get_barrier_semaphore()
    peers = [at_y(j) for j in range(1, ny)] + [at_c]
    peers += [at_x(j) for j in range(1, nx)] + [at_z(j) for j in range(1, nz)]
    for to in peers:
        pl.semaphore_signal(barrier, inc=1, device_id=to, device_id_type=MESH)

    tables = [
        pltpu.make_async_copy(src, dst, in_sem.at[5 + i])
        for i, (src, dst) in enumerate(
            ((doc_table, doc_pick), (word_table, word_pick), (live_table, live))
        )
    ]
    for copy in tables:
        copy.start()
    counts_in = pltpu.make_async_copy(counts_hbm.at[0, 0], cbuf.at[pl.ds(0, slots)], in_sem.at[2])
    counts_in.start()
    doc_in = [
        pltpu.make_async_copy(
            doc_hbm.at[pl.ds((2 * q + c) * share, share)], dbuf.at[q], doc_sem.at[q]
        )
        for q in range(ny)
    ]
    for copy in doc_in:
        copy.start()
    noise_in = pltpu.make_async_copy(noise_hbm, noise_ref, in_sem.at[3])
    noise_in.start()

    def word_rows(jx, jz):
        row = (lax.rem(x - jx + nx, nx) * nz + lax.rem(z - jz + nz, nz)) * share
        return pl.ds(pl.multiple_of(row, share), share)

    def word_block(jx):
        return pl.ds(pl.multiple_of(lax.rem(x - jx + nx, nx) * rows_x, rows_x), rows_x)

    def shard(jx, jz):
        return prob.at[c, word_rows(jx, jz)]

    word_in.wait()
    mass_in.wait()
    prob[c, word_rows(0, 0), :] = (word_ref[...] / mass_ref[...]).astype(jnp.bfloat16)
    pl.semaphore_wait(barrier, len(peers))

    pz = {j: remote(shard(0, 0), shard(0, 0), pz_s.at[j], pz_r.at[j], at_z(j)) for j in range(1, nz)}
    px = {
        (jx, jz): remote(shard(0, jz), shard(0, jz), px_s.at[jx, jz], px_r.at[jx, jz], at_x(jx))
        for jx in range(1, nx)
        for jz in range(nz)
    }
    pc = [
        remote(prob.at[c, word_block(jx)], prob.at[c, word_block(jx)], pc_s.at[jx], pc_r.at[jx], at_c)
        for jx in range(nx)
    ]
    for j in near_first(nz):
        pz[j].start()
    for jx in far_first(nx):
        px[jx, 0].start()

    for copy in tables:
        copy.wait()
    lane = lax.broadcasted_iota(jnp.int32, (1, 128), 1)
    slot_of = jnp.full((1, 128), slots, jnp.int32)
    for s in range(slots):
        key = doc_pick[0, 0, s] * wblocks + word_pick[0, 0, s]
        use = jnp.where(s < live[0, 0], s, slots)
        slot_of = jnp.where(lane == key, use, slot_of)
    slot_vm[...] = slot_of
    slot_in = pltpu.make_async_copy(slot_vm, slot_ref, in_sem.at[4])
    slot_in.start()

    for copy in doc_in:
        copy.wait()
    for h in range(CHAINS):
        for q in range(ny):
            gall[q, c, h] = dbuf[q, h * sub:(h + 1) * sub, :].astype(jnp.bfloat16)
        gam[h] = dbuf[y, h * sub:(h + 1) * sub, :]

    for jz in near_first(nz):
        remote(shard(0, jz), shard(0, jz), pz_s.at[jz], pz_r.at[jz], at_z(jz)).wait_recv()
        for jx in far_first(nx):
            px[jx, jz].start()
    pc[0].start()

    counts_in.wait()
    slot_in.wait()
    cbuf[slots] = jnp.zeros((block, block), jnp.int32)
    pairs = block // share // 2

    def place(t, _):
        d, w = t // wblocks, lax.rem(t, wblocks)
        slot = slot_ref[0, t]
        col = pl.ds(pl.multiple_of(w * block, block), block)
        for k in range(pairs):
            for other in range(2):
                core = sib if other else c
                piece = cbuf[slot, pl.ds(pl.multiple_of((2 * k + core) * share, share), share), :]
                piece = piece.astype(jnp.float32).astype(jnp.bfloat16)
                for h in range(CHAINS):
                    row = pl.ds(pl.multiple_of((d * pairs + k) * sub, sub), sub)
                    val = piece[h * sub:(h + 1) * sub]
                    if other:
                        cnt_sib[h, row, col] = val
                    else:
                        cnt[c, h, row, col] = val
        return 0

    lax.fori_loop(0, slots, place, 0)
    cnt_go = remote(cnt_sib, cnt.at[c], cnt_sem.at[0], cnt_sem.at[1], at_c)
    cnt_go.start()

    def turn(w, _):
        row = pl.ds(pl.multiple_of(w * block, block), block)
        for d in range(slots // wblocks):
            tile = cbuf[slot_ref[0, d * wblocks + w]].astype(jnp.float32)
            cnt_t[row, d * block:(d + 1) * block] = tile.T.astype(jnp.bfloat16)
        return 0

    lax.fori_loop(0, wblocks, turn, 0)

    def chain_gamma(h):
        return jnp.concatenate([gall[q, c, h] for q in range(ny)], axis=0)

    both = jnp.concatenate([chain_gamma(h) for h in range(CHAINS)], axis=0)

    def first_sums(side, jx, first):
        words = word_block(jx)
        p = prob[side, words, :]
        n = jnp.concatenate([cnt[side, h, :, words] for h in range(CHAINS)], axis=0)
        ratios = (n.astype(jnp.float32) / nt_dot(both, p)).astype(jnp.bfloat16)
        add = jnp.dot(ratios, p, preferred_element_type=jnp.float32)
        for h in range(CHAINS):
            if first:
                part[h] = add[h * docs:(h + 1) * docs]
            else:
                part[h] += add[h * docs:(h + 1) * docs]

    def sib_sums(jx):
        theirs = prob.at[sib, word_block(jx)]
        remote(theirs, theirs, pc_s.at[jx], pc_r.at[jx], at_c).wait_recv()
        first_sums(sib, jx, False)

    first_sums(c, 0, True)
    remote(cnt_sib, cnt.at[sib], cnt_sem.at[0], cnt_sem.at[1], at_c).wait_recv()
    sib_sums(0)
    before = None
    for jx in near_first(nx):
        for jz in [0] + near_first(nz):
            remote(shard(jx, jz), shard(jx, jz), px_s.at[jx, jz], px_r.at[jx, jz], at_x(jx)).wait_recv()
        pc[jx].start()
        first_sums(c, jx, False)
        if before is not None:
            sib_sums(before)
        before = jx
    sib_sums(before)

    chunk = min(512, panel)

    def partial_sums(h):
        g = chain_gamma(h)
        total = None
        for side in range(2):
            for k in range(panel // chunk):
                words = pl.ds(k * chunk, chunk)
                p = prob[side, words, :]
                n = cnt[side, h, :, words].astype(jnp.float32)
                ratios = (n / nt_dot(g, p)).astype(jnp.bfloat16)
                add = jnp.dot(ratios, p, preferred_element_type=jnp.float32)
                total = add if total is None else total + add
        part[h] = total

    def doc_rows(j):
        return pl.ds(pl.multiple_of(lax.rem(y + j + ny, ny) * sub, sub), sub)

    def send_sums(h, j):
        to = lax.rem(y + j, ny)
        return remote(part_go.at[h, to], got.at[h, j], s_s.at[h, j], s_r.at[h, j], at_y(j))

    def send_scale(h, j):
        to = lax.rem(y + j, ny)
        return remote(part_sc.at[h, to], got_sc.at[h, j], sc_s.at[h, j], sc_r.at[h, j], at_y(j))

    def pack_sums(h):
        for q in range(ny):
            rows = slice(q * sub, (q + 1) * sub)
            here = part[h, rows, :] * gall[q, c, h].astype(jnp.float32)
            store_packed(part_go.at[h, q], part_sc.at[h, q], here)

    def send_gamma(h, j):
        own = gall.at[y, c, h]
        return remote(own, own, g_s.at[h, j], g_r.at[h, j], at_y(j))

    def wait_gamma(h, j):
        theirs = gall.at[lax.rem(y - j + ny, ny), c, h]
        remote(theirs, theirs, g_s.at[h, j], g_r.at[h, j], at_y(j)).wait_recv()

    for it in range(ITERS):
        for h in range(CHAINS):
            if it:
                for j in near_first(ny):
                    wait_gamma(h, j)
                for j in range(1, ny):
                    send_sums(h, j).wait_send()
                    send_scale(h, j).wait_send()
                partial_sums(h)
            pack_sums(h)
            for j in far_first(ny):
                send_scale(h, j).start()
            for j in far_first(ny):
                send_sums(h, j).start()
        for h in range(CHAINS):
            total = None
            for j in far_first(ny):
                send_scale(h, j).wait_recv()
                send_sums(h, j).wait_recv()
                add = unpack(got.at[h, j], got_sc.at[h, j])
                total = add if total is None else total + add
            total = part[h, doc_rows(0), :] + total / gall[y, c, h].astype(jnp.float32)
            gam[h] = ALPHA_PRIOR + gam[h] * total
            if it:
                for j in range(1, ny):
                    send_gamma(h, j).wait_send()
            gall[y, c, h] = gam[h].astype(jnp.bfloat16)
            for j in far_first(ny):
                send_gamma(h, j).start()

    final = jnp.concatenate([gam[h] for h in range(CHAINS)], axis=0)
    tot_y[0] = jnp.sum(final - ALPHA_PRIOR, axis=0, keepdims=True)

    def send_ty(j):
        return remote(tot_y.at[0], tot_y.at[j], ty_s.at[j], ty_r.at[j], at_y(j))

    for j in far_first(ny):
        send_ty(j).start()
    doc_out[...] = final / (jnp.sum(final, axis=1, keepdims=True) / topics)

    def give(h):
        mine = gall.at[:, c, h]
        return remote(mine, mine, gc_s.at[h], gc_r.at[h], at_c)

    def wait_give(h):
        theirs = gall.at[:, sib, h]
        remote(theirs, theirs, gc_s.at[h], gc_r.at[h], at_c).wait_recv()

    for h in range(CHAINS):
        for j in near_first(ny):
            wait_gamma(h, j)
        give(h).start()
    total = tot_y[0]
    for j in near_first(ny):
        send_ty(j).wait_recv()
        total = total + tot_y[j]
    tot_c[0] = total
    send_tc = remote(tot_c.at[0], tot_c.at[1], tc_s, tc_r, at_c)
    send_tc.start()
    for h in range(CHAINS):
        wait_give(h)

    def z_rows(j):
        return pl.ds(pl.multiple_of(lax.rem(z + j, nz) * share, share), share)

    def send_hx(jx, jz):
        return remote(
            hits_go.at[jx, lax.rem(z + jz, nz)], got_x.at[jx, jz],
            hx_s.at[jx, jz], hx_r.at[jx, jz], at_x(jx),
        )

    def send_xs(jx):
        return remote(hits_sc.at[jx], got_xs.at[jx], xs_s.at[jx], xs_r.at[jx], at_x(jx))

    def send_zs(j):
        return remote(sum_sc.at[j], got_zs.at[j], zs_s.at[j], zs_r.at[j], at_z(j))

    def send_hz(j):
        return remote(sum_go.at[j], got_z.at[j], hz_s.at[j], hz_r.at[j], at_z(j))

    def send_tx(j):
        return remote(tot_x.at[0], tot_x.at[j], tx_s.at[j], tx_r.at[j], at_x(j))

    def send_tz(j):
        return remote(tot_z.at[0], tot_z.at[j], tz_s.at[j], tz_r.at[j], at_z(j))

    send_tc.wait_recv()
    tot_x[0] = tot_c[0] + tot_c[1]
    for j in far_first(nx):
        send_tx(j).start()
    gamma_all = gall[...].reshape(2 * CHAINS * docs, topics)
    z_order, x_order = far_first(nz) + [0], far_first(nx)
    early = nz // 2
    for jx in x_order + [0]:
        words = word_block(nx - jx)
        p = prob[c, words, :]
        ratios = (cnt_t[words, :].astype(jnp.float32) / nt_dot(p, gamma_all)).astype(jnp.bfloat16)
        found = jnp.dot(ratios, gamma_all, preferred_element_type=jnp.float32) * p.astype(jnp.float32)
        if not jx:
            hits[...] = found
        else:
            for q in range(nz):
                store_packed(hits_go.at[jx, q], hits_sc.at[jx, q], found[q * share:(q + 1) * share])
            send_xs(jx).start()
            if jx == x_order[0]:
                for jz in z_order[:early]:
                    send_hx(jx, jz).start()
            if jx == x_order[-1]:
                for jz in z_order:
                    for to in x_order:
                        if to != x_order[0] or jz not in z_order[:early]:
                            send_hx(to, jz).start()

    total = tot_x[0]
    for j in near_first(nx):
        send_tx(j).wait_recv()
        total = total + tot_x[j]
    tot_z[0] = total
    for j in far_first(nz):
        send_tz(j).start()

    for jx in far_first(nx):
        send_xs(jx).wait_recv()
    for jz in z_order:
        total = hits[z_rows(jz), :]
        for jx in range(1, nx):
            send_hx(jx, jz).wait_recv()
            total = total + unpack(got_x.at[jx, jz], got_xs.at[jx, lax.rem(z + jz, nz)])
        if jz:
            store_packed(sum_go.at[jz], sum_sc.at[jz], total)
            send_zs(jz).start()
            send_hz(jz).start()
    reduced = total

    totals = tot_z[0]
    for j in near_first(nz):
        send_tz(j).wait_recv()
        totals = totals + tot_z[j]
    noise_in.wait()
    for j in far_first(nz):
        send_zs(j).wait_recv()
        send_hz(j).wait_recv()
        reduced = reduced + unpack(got_z.at[j], got_zs.at[j])
    word = word_ref[...]
    probs = word / mass_ref[...]
    counted = reduced * (probs / prob[c, word_rows(0, 0), :].astype(jnp.float32))
    drift = BETA_PRIOR - word + GRAD_SCALE * (counted - totals * probs)
    word_out[...] = jnp.abs(word + HALF_STEP * drift + jnp.sqrt(word) * noise_ref[...])

    for j in range(1, nz):
        pz[j].wait_send()
        send_hz(j).wait_send()
        send_zs(j).wait_send()
        send_tz(j).wait_send()
    for jx in range(1, nx):
        send_tx(jx).wait_send()
        send_xs(jx).wait_send()
        for jz in range(nz):
            px[jx, jz].wait_send()
            send_hx(jx, jz).wait_send()
    for jx in range(nx):
        pc[jx].wait_send()
    cnt_go.wait_send()
    send_tc.wait_send()
    for h in range(CHAINS):
        give(h).wait_send()
        for j in range(1, ny):
            send_sums(h, j).wait_send()
            send_scale(h, j).wait_send()
            send_gamma(h, j).wait_send()
    for j in range(1, ny):
        send_ty(j).wait_send()


def shards(counts, tile_doc, tile_word, tile_live, doc_init, topic_word, topic_mass, noise):
    topics = topic_mass.shape[0]
    slots, block = counts.shape[2], counts.shape[3]
    n_dp, n_vocab = lax.axis_size("dp"), lax.axis_size("vocab")
    nx = X_CHIPS
    nz, ny = n_dp // nx, n_vocab // 2
    share = topic_word.shape[0]
    panel = share * n_dp
    sub = share // CHAINS
    docs = ny * sub

    f32, bf16, i32, dma = jnp.float32, jnp.bfloat16, jnp.int32, pltpu.SemaphoreType.DMA
    vmem = pl.BlockSpec(memory_space=pltpu.VMEM)
    hbm = pl.BlockSpec(memory_space=pl.ANY)
    return pl.pallas_call(
        functools.partial(body, nx, nz, ny, share),
        out_shape=(
            jax.ShapeDtypeStruct((share, topics), f32),
            jax.ShapeDtypeStruct((share, topics), f32),
        ),
        in_specs=[hbm, hbm, hbm, hbm, hbm, hbm, hbm, hbm],
        out_specs=(vmem, vmem),
        scratch_shapes=[
            pltpu.SMEM((1, 1, slots), i32),
            pltpu.SMEM((1, 1, slots), i32),
            pltpu.SMEM((1, 1), i32),
            pltpu.VMEM((1, 128), jnp.int32),
            pltpu.SMEM((1, 128), jnp.int32),
            pltpu.VMEM((slots + 1, block, block), jnp.int32),
            pltpu.VMEM((ny, share, topics), f32),
            pltpu.VMEM((share, topics), f32),
            pltpu.VMEM((1, topics), f32),
            pltpu.VMEM((share, topics), f32),
            pltpu.VMEM((2, CHAINS, docs, panel), bf16),
            pltpu.VMEM((CHAINS, docs, panel), bf16),
            pltpu.VMEM((panel, 2 * CHAINS * docs), bf16),
            pltpu.VMEM((2, panel, topics), bf16),
            pltpu.VMEM((ny, 2, CHAINS, sub, topics), bf16),
            pltpu.VMEM((CHAINS, sub, topics), f32),
            pltpu.VMEM((CHAINS, docs, topics), f32),
            pltpu.VMEM((CHAINS, ny, sub // 2, topics), i32),
            pltpu.VMEM((CHAINS, ny, 1, topics), i32),
            pltpu.VMEM((CHAINS, ny, sub // 2, topics), i32),
            pltpu.VMEM((CHAINS, ny, 1, topics), i32),
            pltpu.VMEM((nz * share, topics), f32),
            pltpu.VMEM((nx, nz, share // 2, topics), i32),
            pltpu.VMEM((nx, nz, 1, topics), i32),
            pltpu.VMEM((nx, nz, share // 2, topics), i32),
            pltpu.VMEM((nx, nz, 1, topics), i32),
            pltpu.VMEM((nz, share // 2, topics), i32),
            pltpu.VMEM((nz, 1, topics), i32),
            pltpu.VMEM((nz, share // 2, topics), i32),
            pltpu.VMEM((nz, 1, topics), i32),
            pltpu.VMEM((ny, 1, topics), f32),
            pltpu.VMEM((2, 1, topics), f32),
            pltpu.VMEM((nx, 1, topics), f32),
            pltpu.VMEM((nz, 1, topics), f32),
            dma((8,)), dma((ny,)), dma((2,)),
            dma((nz,)), dma((nz,)), dma((nx, nz)), dma((nx, nz)), dma((nx,)), dma((nx,)),
            dma((CHAINS, ny)), dma((CHAINS, ny)), dma((CHAINS, ny)), dma((CHAINS, ny)),
            dma((CHAINS, ny)), dma((CHAINS, ny)),
            dma((CHAINS,)), dma((CHAINS,)),
            dma((nx, nz)), dma((nx, nz)), dma((nx,)), dma((nx,)),
            dma((nz,)), dma((nz,)), dma((nz,)), dma((nz,)),
            dma((ny,)), dma((ny,)), dma, dma, dma((nx,)), dma((nx,)), dma((nz,)), dma((nz,)),
        ],
        compiler_params=pltpu.CompilerParams(
            collective_id=0, has_side_effects=True, vmem_limit_bytes=VMEM_LIMIT
        ),
    )(tile_doc, tile_word, tile_live, counts, doc_init, topic_word, topic_mass[None, :], noise)


def solution(mesh):
    return jax.shard_map(
        shards,
        mesh=mesh,
        in_specs=(
            P("dp", "vocab", None, None, None),
            P("dp", "vocab", None),
            P("dp", "vocab", None),
            P("dp", "vocab"),
            P("dp", None),
            P(("vocab", "dp"), None),
            P(),
            P(("vocab", "dp"), None),
        ),
        out_specs=(P(("dp", "vocab"), None), P(("vocab", "dp"), None)),
        check_vma=False,
    )
```
